256 devices in a mesh: dp: 2 (over x_lo), ctx: 32 (over z, y), tp: 4 (over x_hi, core).
Axes of the slice: x: 4 (x_hi: 2, x_lo: 2; x = x_hi * 2 + x_lo), y: 4, z: 8, core: 2. Of those that a mesh axis runs over, the one named last changes fastest.
Arguments:
- query_proj: bfloat16 [2, 8192, 2048], P('dp', 'ctx', 'tp'), may hold values from -6 to 6
- key_proj: bfloat16 [2, 8192, 2048], P('dp', 'ctx', 'tp'), may hold values from -6 to 6
- value_proj: bfloat16 [2, 8192, 2048], P('dp', 'ctx', 'tp'), may hold values from -6 to 6
- filters: float32 [2048, 8192], P('tp', 'ctx'), may hold values from -2 to 2
- w_out: bfloat16 [2048, 2048], P('tp'), may hold values from -0.125 to 0.125
- cotangent: bfloat16 [2, 8192, 2048], P('dp', 'ctx', 'tp'), may hold values from -6 to 6
Outputs:
- output: bfloat16 [2, 8192, 2048], P('dp', 'ctx', 'tp')
- grad_query: bfloat16 [2, 8192, 2048], P('dp', 'ctx', 'tp')
- grad_key: bfloat16 [2, 8192, 2048], P('dp', 'ctx', 'tp')
- grad_value: bfloat16 [2, 8192, 2048], P('dp', 'ctx', 'tp')
- grad_filter: float32 [2048, 8192], P('tp', 'ctx')
- grad_wout: float32 [2048, 2048], P('tp', 'ctx')
The draws below stay inside these ranges and needn't reach their ends.
All inputs are finite; a program needn't handle non-finite values.
Results may differ from the reference program's by a relative error of at most 0.0049.
Values may be sent and summed in bfloat16 or wider, within the bound.
A program may use at most 64 MiB of HBM per device.

```python
import math
import jax
import jax.numpy as jnp
from jax import lax

C = 2048
DOUT = 2048
BATCH = 2
L = 8192


def envelope_norm(rates, length):
    return jnp.sqrt(2.0 * rates / (1.0 - jnp.exp(-2.0 * rates * length)))


def draw_filters(key, part):
    key = jax.random.fold_in(key, 11)
    key_fast, key_slow, key_share, key_taps = jax.random.split(key, 4)
    fast_rates = jnp.exp(jax.random.uniform(key_fast, (C, 1), jnp.float32, math.log(1.0 / 400.0), math.log(1.0 / 40.0)))
    slow_rates = jnp.exp(jax.random.uniform(key_slow, (C, 1), jnp.float32, math.log(0.1 / L), math.log(1.5 / L)))
    slow_share = jax.random.uniform(key_share, (C, 1), jnp.float32, 0.3, 0.7)
    tap_index = jnp.arange(L, dtype=jnp.float32)[None, :]
    fast_part = jnp.exp(-fast_rates * tap_index) * envelope_norm(fast_rates, L) * jnp.sqrt(1.0 - slow_share)
    slow_part = jnp.exp(-slow_rates * tap_index) * envelope_norm(slow_rates, L) * jnp.sqrt(slow_share)
    envelope = fast_part + slow_part
    pattern = jnp.clip(jax.random.normal(key_taps, (C, L), jnp.float32), -5.0, 5.0)
    return jnp.clip(pattern * envelope, -2.0, 2.0).astype(jnp.float32)


def strengthened(drawn, rng, source, target, shards_of, factor):
    def block_of(dim):
        return (jnp.arange(drawn.shape[dim]) // (drawn.shape[dim] // shards_of)).reshape((-1,) + (1,) * (drawn.ndim - 1 - dim))

    one_side = jax.random.permutation(rng, shards_of)[block_of(target)]
    other_side = (block_of(target) + shards_of // 2) % shards_of
    return jnp.where((block_of(source) == one_side) | (block_of(source) == other_side), factor * drawn, drawn)


def block_scale(key, extent, cuts, least, top_value):
    loudness = 1.0
    for dim, parts in cuts:
        heights = jax.random.uniform(jax.random.fold_in(jax.random.fold_in(key, 6), dim), (parts,), jnp.float32, least / len(cuts), top_value / len(cuts))
        loudness = loudness * jnp.repeat(jnp.exp(heights), extent[dim] // parts).reshape((-1,) + (1,) * (len(extent) - 1 - dim))
    return loudness


def centred(stream_key, extent, deviation, most, pieces=(), held_as=jnp.bfloat16):
    drawn = jax.random.normal(stream_key, extent, jnp.float32) * deviation
    if len(pieces) > 0:
        drawn = block_scale(stream_key, extent, pieces, -0.22, 0.18) * drawn
    return jnp.clip(drawn, min=-most, max=most).astype(held_as)


def noise_with(key, shape, deviation, reach, cuts, heavy, held_as=jnp.bfloat16):
    array = deviation * jax.random.normal(key, shape, jnp.float32)
    if cuts:
        array = array * block_scale(key, shape, cuts, -0.22, 0.18)
    return jnp.clip(strengthened(array, jax.random.fold_in(key, 3), *heavy), -reach, reach).astype(held_as)


def setup_inputs(seed: int = 0) -> dict:
    key_list = jax.random.split(jax.random.key(seed), 7)
    return {
        "query_proj": centred(key_list[0], (BATCH, L, C), 1.0, 6.0, ((0, 2), (1, 32), (2, 4))),
        "key_proj": centred(key_list[1], (BATCH, L, C), 1.0, 6.0, ((0, 2), (1, 32), (2, 4))),
        "value_proj": centred(key_list[2], (BATCH, L, C), 1.0, 6.0, ((0, 2), (1, 32), (2, 4))),
        "filters": draw_filters(jax.random.fold_in(key_list[6], 71), 0),
        "w_out": centred(key_list[4], (C, DOUT), C ** -0.5, 0.125, ((0, 4),)),
        "cotangent": noise_with(key_list[5], (BATCH, L, DOUT), 1.0, 6.0, ((0, 2), (1, 32), (2, 4)), (1, 2, 32, 2.75)),
    }


def reference(query_proj, key_proj, value_proj, filters, w_out, cotangent):
    length = query_proj.shape[1]
    length_fft = 2 * length
    filter_spec = jnp.fft.rfft(filters, n=length_fft, axis=1)

    def one_sequence(inputs):
        query_rows, key_rows, value_rows, grad_rows = inputs
        mixed = (key_rows.astype(jnp.float32) * value_rows.astype(jnp.float32)).T
        mixed_spec = jnp.fft.rfft(mixed, n=length_fft, axis=1)
        conv = jnp.fft.irfft(filter_spec * mixed_spec, n=length_fft, axis=1)[:, :length].T.astype(jnp.float32)
        gated = (query_rows.astype(jnp.float32) * conv).astype(jnp.bfloat16)
        output = jnp.dot(gated, w_out, preferred_element_type=jnp.float32).astype(jnp.bfloat16)
        grad_gated = lax.dot_general(grad_rows, w_out, (((1,), (1,)), ((), ())), preferred_element_type=jnp.float32)
        grad_query = (grad_gated * conv).astype(jnp.bfloat16)
        grad_conv = (grad_gated * query_rows.astype(jnp.float32)).T
        grad_spec = jnp.fft.rfft(grad_conv, n=length_fft, axis=1)
        grad_mixed = jnp.fft.irfft(jnp.conj(filter_spec) * grad_spec, n=length_fft, axis=1)[:, :length].T.astype(jnp.float32)
        filter_term = jnp.fft.irfft(grad_spec * jnp.conj(mixed_spec), n=length_fft, axis=1)[:, :length].astype(jnp.float32)
        grad_key = (grad_mixed * value_rows.astype(jnp.float32)).astype(jnp.bfloat16)
        grad_value = (grad_mixed * key_rows.astype(jnp.float32)).astype(jnp.bfloat16)
        weight_term = lax.dot_general(gated, grad_rows, (((0,), (0,)), ((), ())), preferred_element_type=jnp.float32)
        return (output, grad_query, grad_key, grad_value, filter_term, weight_term)
    results = lax.map(one_sequence, (query_proj, key_proj, value_proj, cotangent))
    output, grad_query, grad_key, grad_value, filter_terms, weight_terms = results
    factor = 1.0 / math.sqrt(BATCH * L)
    grad_filter = lax.optimization_barrier(jnp.sum(filter_terms, axis=0)) * factor
    grad_wout = lax.optimization_barrier(jnp.sum(weight_terms, axis=0)) * factor
    return (output, grad_query, grad_key, grad_value, grad_filter, grad_wout)
```

```python
import math

import jax
import jax.numpy as jnp
from jax import lax
from jax.sharding import PartitionSpec as P


def build_tables(length_fft):
    blocks = length_fft // 128
    outer = jnp.arange(blocks, dtype=jnp.int32)
    inner = jnp.arange(blocks // 2, dtype=jnp.int32)
    column = jnp.arange(128, dtype=jnp.int32)
    first = (outer[:, None] * inner[None, :] % blocks).astype(jnp.float32) * (
        -2.0 * math.pi / blocks
    )
    turned = (outer[:, None] * column[None, :] % length_fft).astype(jnp.float32) * (
        -2.0 * math.pi / length_fft
    )
    second = (column[:, None] * column[None, :] % 128).astype(jnp.float32) * (-2.0 * math.pi / 128)
    return (
        jnp.cos(first),
        jnp.sin(first),
        jnp.cos(turned),
        jnp.sin(turned),
        jnp.cos(second),
        jnp.sin(second),
    )


def product(form, left, right):
    return jnp.einsum(form, left, right, precision=lax.Precision.HIGHEST)


def forward_transform(signal, tables):
    cos_first, sin_first, cos_turn, sin_turn, cos_second, sin_second = tables
    real_one = product("ia,cab->cib", cos_first, signal)
    imag_one = product("ia,cab->cib", sin_first, signal)
    real_two = real_one * cos_turn - imag_one * sin_turn
    imag_two = real_one * sin_turn + imag_one * cos_turn
    real_out = product("cib,bj->cij", real_two, cos_second) - product(
        "cib,bj->cij", imag_two, sin_second
    )
    imag_out = product("cib,bj->cij", real_two, sin_second) + product(
        "cib,bj->cij", imag_two, cos_second
    )
    return (real_out, imag_out)


def inverse_transform(real_in, imag_in, tables, length_fft):
    cos_first, sin_first, cos_turn, sin_turn, cos_second, sin_second = tables
    real_one = product("cij,jb->cib", real_in, cos_second) + product(
        "cij,jb->cib", imag_in, sin_second
    )
    imag_one = product("cij,jb->cib", imag_in, cos_second) - product(
        "cij,jb->cib", real_in, sin_second
    )
    real_two = real_one * cos_turn + imag_one * sin_turn
    imag_two = imag_one * cos_turn - real_one * sin_turn
    result = product("ia,cib->cab", cos_first, real_two) + product(
        "ia,cib->cab", sin_first, imag_two
    )
    return result / length_fft


def exchange(array, axis, split, concat, groups=None):
    return lax.all_to_all(
        array.astype(jnp.bfloat16),
        axis,
        split_axis=split,
        concat_axis=concat,
        axis_index_groups=groups,
        tiled=True,
    ).astype(jnp.float32)


def local(query_proj, key_proj, value_proj, filters, w_out, cotangent):
    query_rows = query_proj[0].astype(jnp.float32)
    key_rows = key_proj[0].astype(jnp.float32)
    value_rows = value_proj[0].astype(jnp.float32)
    positions, channels = query_rows.shape
    seq_devices = lax.axis_size("ctx")
    tp_devices = lax.axis_size("tp")
    inner = 4
    outer = seq_devices // inner
    inner_groups = [[o * inner + i for i in range(inner)] for o in range(outer)]
    outer_groups = [[o * inner + i for o in range(outer)] for i in range(inner)]
    length_fft = 2 * positions * seq_devices
    tables = build_tables(length_fft)
    mixed = (key_rows * value_rows).T
    mixed_chan = exchange(mixed, "ctx", 0, 1)
    filter_chan = exchange(filters, "ctx", 0, 1)
    piece = lax.all_gather(cotangent[0], "tp", axis=1, tiled=True)
    grad_gated = lax.dot_general(
        piece, w_out, (((1,), (1,)), ((), ())), preferred_element_type=jnp.float32
    )
    grad_conv = (grad_gated * query_rows).T
    grad_chan = exchange(grad_conv, "ctx", 0, 1)
    local_channels = mixed_chan.shape[0]
    block_shape = (local_channels, length_fft // 256, 128)
    mixed_real, mixed_imag = forward_transform(mixed_chan.reshape(block_shape), tables)
    filter_real, filter_imag = forward_transform(filter_chan.reshape(block_shape), tables)
    conv_real = filter_real * mixed_real - filter_imag * mixed_imag
    conv_imag = filter_real * mixed_imag + filter_imag * mixed_real
    conv_chan = inverse_transform(conv_real, conv_imag, tables, length_fft).reshape(
        local_channels, -1
    )
    conv = exchange(conv_chan, "ctx", 1, 0).T
    gated = (query_rows * conv).astype(jnp.bfloat16)
    partial_terms = jnp.dot(gated, w_out, preferred_element_type=jnp.float32)
    features = partial_terms.shape[1] // tp_devices
    terms = exchange(partial_terms, "tp", 1, 0).reshape(tp_devices, positions, features)
    output = jnp.sum(terms, axis=0).astype(jnp.bfloat16)
    weight_grad = lax.dot_general(
        gated, piece, (((0,), (0,)), ((), ())), preferred_element_type=jnp.float32
    )
    grad_query = (grad_gated * conv).astype(jnp.bfloat16)
    grad_real, grad_imag = forward_transform(grad_chan.reshape(block_shape), tables)
    back_real = filter_real * grad_real + filter_imag * grad_imag
    back_imag = filter_real * grad_imag - filter_imag * grad_real
    taps_real = grad_real * mixed_real + grad_imag * mixed_imag
    taps_imag = grad_imag * mixed_real - grad_real * mixed_imag
    mixed_grad_chan = inverse_transform(back_real, back_imag, tables, length_fft).reshape(
        local_channels, -1
    )
    filter_grad_chan = inverse_transform(taps_real, taps_imag, tables, length_fft).reshape(
        local_channels, -1
    )
    grad_mixed = exchange(mixed_grad_chan, "ctx", 1, 0).T
    filter_grad_back = exchange(filter_grad_chan, "ctx", 1, 0)
    grad_key = (grad_mixed * value_rows).astype(jnp.bfloat16)
    grad_value = (grad_mixed * key_rows).astype(jnp.bfloat16)
    factor = 1.0 / math.sqrt(lax.axis_size("dp") * positions * seq_devices)
    swap = [(0, 1), (1, 0)]
    other = lax.ppermute(filter_grad_back.astype(jnp.bfloat16), "dp", swap).astype(jnp.float32)
    grad_filter = (filter_grad_back + other) * factor
    wide = weight_grad.shape[1] // seq_devices
    pieces = weight_grad.reshape(channels, outer, inner, wide).transpose(2, 1, 0, 3)
    pieces = exchange(pieces, "ctx", 0, 0, inner_groups)
    pieces = jnp.sum(pieces, axis=0)
    pieces = exchange(pieces, "ctx", 0, 0, outer_groups)
    summed = jnp.sum(pieces, axis=0)
    grad_wout = (summed + lax.ppermute(summed, "dp", swap)) * factor
    return (
        output[None],
        grad_query[None],
        grad_key[None],
        grad_value[None],
        grad_filter,
        grad_wout,
    )


def solution(mesh):
    in_specs = (
        P("dp", "ctx", "tp"),
        P("dp", "ctx", "tp"),
        P("dp", "ctx", "tp"),
        P("tp", "ctx"),
        P("tp", None),
        P("dp", "ctx", "tp"),
    )
    out_specs = (
        P("dp", "ctx", "tp"),
        P("dp", "ctx", "tp"),
        P("dp", "ctx", "tp"),
        P("dp", "ctx", "tp"),
        P("tp", "ctx"),
        P("tp", "ctx"),
    )
    return jax.shard_map(local, mesh=mesh, in_specs=in_specs, out_specs=out_specs, check_vma=False)
```

```python
import functools
import math

import jax
import jax.numpy as jnp
import ml_dtypes
import numpy as np
from jax import lax
from jax.experimental import pallas as pl
from jax.experimental.pallas import tpu as pltpu
from jax.sharding import PartitionSpec as P

MESH = pl.DeviceIdType.MESH
F32 = jnp.float32
BF16 = jnp.bfloat16

DP = 2
SEQ = 32
ZN = 8
YN = 4
GROUP = DP * SEQ
CH = 8
BLOCKS = 64
LANES = 128
LENGTH = BLOCKS * LANES
ROWS = BLOCKS * CH
STEP = 256


def halves(table):
    high = table.astype(ml_dtypes.bfloat16)
    low = (table - high.astype(np.float64)).astype(ml_dtypes.bfloat16)
    return np.stack([high, low])


@functools.lru_cache(maxsize=None)
def tables():
    k1 = np.arange(BLOCKS)[:, None].astype(np.float64)
    turn = 2 * math.pi * k1 + math.pi / 2
    outer = turn * np.arange(BLOCKS)[None, :] / BLOCKS
    eye = np.eye(CH)
    stage_one = np.concatenate([np.kron(np.cos(outer), eye), np.kron(-np.sin(outer), eye)], axis=0)
    angle = np.repeat(turn * np.arange(LANES)[None, :] / LENGTH, CH, axis=0)
    twiddle = np.stack([np.cos(angle), -np.sin(angle)]).astype(np.float32)
    lane = np.arange(LANES)
    inner = 2 * math.pi * ((lane[:, None] * lane[None, :]) % LANES) / LANES
    c, s = np.cos(inner), np.sin(inner)
    stage_two = np.block([[c, -s], [s, c]])
    stage_two_back = np.block([[c, s], [-s, c]])
    return (
        halves(stage_one),
        halves(stage_one.T),
        np.concatenate([halves(stage_two), halves(stage_two_back)]),
        twiddle,
    )


def dot(a, b):
    return jnp.dot(a, b, preferred_element_type=F32)


def split(x):
    high = x.astype(BF16)
    return high, (x - high.astype(F32)).astype(BF16)


def kernel(
    factor,
    q_ref, k_ref, v_ref, f_ref, w_ref, cot_ref, one_hbm, back_hbm, two_hbm, tw_hbm,
    out_ref, gq_ref, gk_ref, gv_ref, gf_ref, gw_ref,
    one, back, two, tw,
    mix_send, mix_recv, fil_send, fil_recv, gc_send, gc_recv,
    conv_send, conv_recv, gm_send, gm_recv, fg_send, fg_recv,
    cot_all, cot_t, gg, xcat, spec_m, spec_f, spec_g, v_hi, v_lo,
    gated, w_send, w_recv, z_send, z_recv, d_send, d_recv,
    core_send, core_recv, x_send, x_recv, own,
    table_sem, send_sem, recv_sem, tp_send, tp_recv, y_ssem, y_rsem, z_ssem, z_rsem, d_sem,
):
    d = lax.axis_index("dp")
    j = lax.axis_index("ctx")
    t = lax.axis_index("tp")
    z = j // YN
    y = lax.rem(j, YN)
    core = lax.rem(t, 2)
    hi_x = t // 2
    me = d * SEQ + j
    t_core = hi_x * 2 + (1 - core)
    t_x = (1 - hi_x) * 2 + core
    t_far = (1 - hi_x) * 2 + (1 - core)

    def peer(offset):
        p = lax.rem(me + offset, GROUP)
        return p, {"dp": p // SEQ, "ctx": lax.rem(p, SEQ)}

    local = []
    for i, (src, dst) in enumerate(((one_hbm, one), (two_hbm, two), (tw_hbm, tw), (back_hbm, back))):
        copy = pltpu.make_async_copy(src, dst, table_sem.at[i])
        copy.start()
        local.append(copy)

    barrier = pltpu.get_barrier_semaphore()

    def greet(i, carry):
        pl.semaphore_signal(barrier, inc=1, device_id=peer(i)[1], device_id_type=MESH)
        return carry

    lax.fori_loop(1, GROUP, greet, 0)
    for other in (t_core, t_x):
        pl.semaphore_signal(barrier, inc=1, device_id={"tp": other}, device_id_type=MESH)

    def to_chunks(rows):
        count = rows.shape[0] // CH
        parts = [rows[:, h * LANES : (h + 1) * LANES].reshape(count, CH, LANES) for h in range(2)]
        return jnp.concatenate(parts, axis=1).astype(BF16)

    def from_chunks(ref):
        chunks = ref[...].astype(F32)
        parts = [chunks[:, h * CH : (h + 1) * CH, :].reshape(GROUP * CH, LANES) for h in range(2)]
        return jnp.concatenate(parts, axis=1)

    mix_send[...] = to_chunks((k_ref[...].astype(F32) * v_ref[...].astype(F32)).T)
    half = SEQ * CH
    fil_send[...] = to_chunks(f_ref[pl.ds(pl.multiple_of(d * half, half), half), :])
    mix_recv[me] = mix_send[me]
    fil_recv[j] = fil_send[j]
    cot_all[t] = cot_ref[...]

    pl.semaphore_wait(barrier, GROUP + 1)

    def remote(src, dst, ssem, rsem, device):
        return pltpu.make_async_remote_copy(
            src_ref=src, dst_ref=dst, send_sem=ssem, recv_sem=rsem, device_id=device, device_id_type=MESH
        )

    cot_core = remote(cot_ref, cot_all.at[t], tp_send.at[0], tp_recv.at[0], {"tp": t_core})
    cot_x = remote(cot_ref, cot_all.at[t], tp_send.at[1], tp_recv.at[1], {"tp": t_x})
    cot_x.start()
    cot_core.start()

    def scatter(src, dst, index, same):
        def start(i, carry):
            p, device = peer(i)
            chunk = lax.rem(p, SEQ) if same else p
            remote(src.at[chunk], dst.at[me], send_sem.at[index], recv_sem.at[index], device).start()
            return carry

        lax.fori_loop(1, GROUP, start, 0)

    def arrived(dst, index, count=GROUP - 1):
        part = dst.at[pl.ds(0, count)]
        remote(part, part, send_sem.at[index], recv_sem.at[index], {"tp": t_core}).wait_recv()

    def left(dst, index, count=GROUP - 1):
        part = dst.at[pl.ds(0, count)]
        remote(part, part, send_sem.at[index], recv_sem.at[index], {"tp": t_core}).wait_send()

    scatter(mix_send, mix_recv, 0, False)

    def start_filter(i, carry):
        p = lax.rem(j + i, SEQ)
        remote(fil_send.at[p], fil_recv.at[j], send_sem.at[1], recv_sem.at[1], {"ctx": p}).start()
        return carry

    lax.fori_loop(1, SEQ, start_filter, 0)

    width = cot_ref.shape[1]

    def grad_part(o):
        weights = w_ref[:, pl.ds(pl.multiple_of(o * width, width), width)]
        return lax.dot_general(
            cot_all[o], weights, (((1,), (1,)), ((), ())), preferred_element_type=F32
        )

    def turn(o):
        rows = pl.ds(pl.multiple_of(o * width, width), width)
        cot_t[rows, :] = cot_all[o].astype(F32).T.astype(BF16)

    gg[...] = grad_part(t)
    turn(t)
    cot_core.wait_recv()
    gg[...] += grad_part(t_core)
    turn(t_core)
    cot_x.wait_recv()
    forward = remote(
        cot_all.at[t_x], cot_all.at[t_x], tp_send.at[2], tp_recv.at[2], {"tp": t_core}
    )
    forward.start()
    gg[...] += grad_part(t_x)
    forward.wait_recv()
    total = gg[...] + grad_part(t_far)
    gg[...] = total
    gc_send[...] = to_chunks((total * q_ref[...].astype(F32)).T)
    gc_recv[me] = gc_send[me]
    scatter(gc_send, gc_recv, 2, False)
    turn(t_x)
    turn(t_far)

    def rows_of(i, base=0):
        return pl.ds(pl.multiple_of(base + i * STEP, STEP), STEP)

    def forward_transform(recv, count, spec):
        for b in range(count):
            xcat[:, b * LANES : (b + 1) * LANES] = recv[b * SEQ : (b + 1) * SEQ].reshape(ROWS, LANES)

        def body(i, carry):
            x = xcat[:, : count * LANES]
            real = dot(one[0, rows_of(i), :], x) + dot(one[1, rows_of(i), :], x)
            imag = dot(one[0, rows_of(i, ROWS), :], x) + dot(one[1, rows_of(i, ROWS), :], x)
            c, s = tw[0, rows_of(i), :], tw[1, rows_of(i), :]
            for b in range(count):
                re = real[:, b * LANES : (b + 1) * LANES]
                im = imag[:, b * LANES : (b + 1) * LANES]
                high, low = split(jnp.concatenate([re * c - im * s, re * s + im * c], axis=1))
                spec[b, rows_of(i), :] = dot(high, two[0]) + dot(low, two[0]) + dot(high, two[1])
            return carry

        lax.fori_loop(0, ROWS // STEP, body, 0)

    def inverse_transform(product, count, send):
        def first(i, carry):
            c, s = tw[0, rows_of(i), :], tw[1, rows_of(i), :]
            for b in range(count):
                high, low = split(jnp.concatenate(product(b, rows_of(i)), axis=1))
                u = dot(high, two[2]) + dot(low, two[2]) + dot(high, two[3])
                re, im = u[:, :LANES], u[:, LANES:]
                lanes = slice(b * LANES, (b + 1) * LANES)
                high, low = split(re * c + im * s)
                v_hi[rows_of(i), lanes] = high
                v_lo[rows_of(i), lanes] = low
                high, low = split(im * c - re * s)
                v_hi[rows_of(i, ROWS), lanes] = high
                v_lo[rows_of(i, ROWS), lanes] = low
            return carry

        lax.fori_loop(0, ROWS // STEP, first, 0)

        def second(i, carry):
            high, low = v_hi[:, : count * LANES], v_lo[:, : count * LANES]
            table = back[0, rows_of(i), :]
            result = dot(table, high) + dot(table, low) + dot(back[1, rows_of(i), :], high)
            result = (result * (1.0 / LENGTH)).astype(BF16)
            chunks = STEP // (2 * CH)
            for b in range(count):
                part = result[:, b * LANES : (b + 1) * LANES].reshape(chunks, 2 * CH, LANES)
                send[pl.ds(b * SEQ + i * chunks, chunks)] = part
            return carry

        lax.fori_loop(0, ROWS // STEP, second, 0)

    def pair(ref, b, rows):
        return ref[b, rows, :LANES], ref[b, rows, LANES:]

    def conv_product(b, rows):
        fr, fi = pair(spec_f, 0, rows)
        mr, mi = pair(spec_m, b, rows)
        return fr * mr - fi * mi, fr * mi + fi * mr

    def grad_product(b, rows):
        fr, fi = pair(spec_f, 0, rows)
        gr, gi = pair(spec_g, b, rows)
        return fr * gr + fi * gi, fr * gi - fi * gr

    def taps_product(_, rows):
        real, imag = 0.0, 0.0
        for b in range(DP):
            mr, mi = pair(spec_m, b, rows)
            gr, gi = pair(spec_g, b, rows)
            real += gr * mr + gi * mi
            imag += gi * mr - gr * mi
        return real, imag

    for copy in local:
        copy.wait()
    arrived(mix_recv, 0)
    forward_transform(mix_recv, DP, spec_m)
    arrived(fil_recv, 1, SEQ - 1)
    forward_transform(fil_recv, 1, spec_f)
    inverse_transform(conv_product, DP, conv_send)
    conv_recv[me] = conv_send[me]
    scatter(conv_send, conv_recv, 3, False)
    arrived(gc_recv, 2)
    forward_transform(gc_recv, DP, spec_g)
    inverse_transform(grad_product, DP, gm_send)
    gm_recv[me] = gm_send[me]
    scatter(gm_send, gm_recv, 4, False)
    inverse_transform(taps_product, 1, fg_send)
    fg_recv[me] = fg_send[j]
    scatter(fg_send, fg_recv, 5, True)

    arrived(conv_recv, 3)
    conv = from_chunks(conv_recv).T
    gq_ref[...] = (gg[...] * conv).astype(BF16)
    gated[...] = (q_ref[...].astype(F32) * conv).astype(BF16)

    features = gw_ref.shape[1]
    channels = gw_ref.shape[0]
    for o in range(4):
        term = dot(cot_t[o * width : (o + 1) * width, :], gated[...])
        for piece in range(width // features):
            part = term[piece * features : (piece + 1) * features, :].astype(BF16)
            w_send[piece % YN, o * 2 + piece // YN] = part
    y_copies = []
    for step in (2, 1, 3):
        to = lax.rem(y + step, YN)
        copy = remote(
            w_send.at[to], w_recv.at[step - 1], y_ssem.at[step - 1], y_rsem.at[step - 1],
            {"ctx": z * YN + to},
        )
        copy.start()
        y_copies.append(copy)

    def partial(o):
        return dot(gated[...], w_ref[:, pl.ds(pl.multiple_of(o * width, width), width)])

    core_send[0] = partial(t_far)
    core_send[1] = partial(t_core)
    core_copy = remote(core_send, core_recv, tp_send.at[3], tp_recv.at[3], {"tp": t_core})
    core_copy.start()
    other_x = partial(t_x)
    own[...] = partial(t)
    core_copy.wait_recv()
    x_send[...] = (other_x + core_recv[0]).astype(BF16)
    x_copy = remote(x_send, x_recv, tp_send.at[4], tp_recv.at[4], {"tp": t_x})
    x_copy.start()

    arrived(gm_recv, 4)
    grad_mixed = from_chunks(gm_recv).T
    gk_ref[...] = (grad_mixed * v_ref[...].astype(F32)).astype(BF16)
    gv_ref[...] = (grad_mixed * k_ref[...].astype(F32)).astype(BF16)
    arrived(fg_recv, 5)
    gf_ref[...] = from_chunks(fg_recv) * factor

    x_copy.wait_recv()
    out_ref[...] = (own[...] + core_recv[1] + x_recv[...].astype(F32)).astype(BF16)

    for copy in y_copies:
        copy.wait_recv()

    def reduce_y(i, carry):
        value = w_send[y, i].astype(F32)
        for slot in range(YN - 1):
            value += w_recv[slot, i].astype(F32)
        z_send[i] = value.astype(BF16)
        return carry

    lax.fori_loop(0, ZN, reduce_y, 0)
    z_recv[z] = z_send[z]
    z_copies = []
    for step in (4, 3, 5, 2, 6, 1, 7):
        to = lax.rem(z + step, ZN)
        copy = remote(
            z_send.at[to], z_recv.at[z], z_ssem.at[step - 1], z_rsem.at[step - 1],
            {"ctx": to * YN + y},
        )
        copy.start()
        z_copies.append(copy)
    for copy in z_copies:
        copy.wait_recv()
    value = z_recv[0].astype(F32)
    for slot in range(1, ZN):
        value += z_recv[slot].astype(F32)
    d_send[...] = value
    d_copy = remote(d_send, d_recv, d_sem.at[0], d_sem.at[1], {"dp": 1 - d})
    d_copy.start()
    d_copy.wait_recv()
    gw_ref[...] = ((d_send[...] + d_recv[...]) * factor).T

    for copy in (cot_core, cot_x, forward, core_copy, x_copy, d_copy, *y_copies, *z_copies):
        copy.wait_send()
    left(mix_send, 0)
    left(fil_send, 1, SEQ - 1)
    left(gc_send, 2)
    left(conv_send, 3)
    left(gm_send, 4)
    left(fg_recv, 5)


def local(query_proj, key_proj, value_proj, filters, w_out, cotangent):
    positions, channels = query_proj.shape[1:]
    features = w_out.shape[1] // SEQ
    factor = 1.0 / math.sqrt(DP * LENGTH)
    one, back, two, twiddle = (jnp.asarray(table) for table in tables())
    stream = jax.ShapeDtypeStruct((positions, channels), BF16)
    vmem = pl.BlockSpec(memory_space=pltpu.VMEM)
    anywhere = pl.BlockSpec(memory_space=pl.ANY)
    chunks = pltpu.VMEM((GROUP, 2 * CH, LANES), BF16)
    half_chunks = pltpu.VMEM((SEQ, 2 * CH, LANES), BF16)
    wide = w_out.shape[1]
    dma = pltpu.SemaphoreType.DMA
    outs = pl.pallas_call(
        functools.partial(kernel, factor),
        out_shape=(
            stream,
            stream,
            stream,
            stream,
            jax.ShapeDtypeStruct((channels, positions), F32),
            jax.ShapeDtypeStruct((channels, features), F32),
        ),
        in_specs=[vmem] * 6 + [anywhere] * 4,
        out_specs=[vmem] * 6,
        scratch_shapes=[
            pltpu.VMEM(one.shape, BF16),
            pltpu.VMEM(back.shape, BF16),
            pltpu.VMEM(two.shape, BF16),
            pltpu.VMEM(twiddle.shape, F32),
            chunks, chunks, half_chunks, half_chunks, chunks, chunks,
            chunks, chunks, chunks, chunks, half_chunks, chunks,
            pltpu.VMEM((4, positions, channels), BF16),
            pltpu.VMEM((wide, positions), BF16),
            pltpu.VMEM((positions, channels), F32),
            pltpu.VMEM((ROWS, DP * LANES), BF16),
            pltpu.VMEM((DP, ROWS, 2 * LANES), F32),
            pltpu.VMEM((1, ROWS, 2 * LANES), F32),
            pltpu.VMEM((DP, ROWS, 2 * LANES), F32),
            pltpu.VMEM((2 * ROWS, DP * LANES), BF16),
            pltpu.VMEM((2 * ROWS, DP * LANES), BF16),
            pltpu.VMEM((positions, channels), BF16),
            pltpu.VMEM((YN, ZN, features, channels), BF16),
            pltpu.VMEM((YN - 1, ZN, features, channels), BF16),
            pltpu.VMEM((ZN, features, channels), BF16),
            pltpu.VMEM((ZN, features, channels), BF16),
            pltpu.VMEM((features, channels), F32),
            pltpu.VMEM((features, channels), F32),
            pltpu.VMEM((2, positions, channels), F32),
            pltpu.VMEM((2, positions, channels), F32),
            pltpu.VMEM((positions, channels), BF16),
            pltpu.VMEM((positions, channels), BF16),
            pltpu.VMEM((positions, channels), F32),
            dma((4,)), dma((6,)), dma((6,)), dma((5,)), dma((5,)),
            dma((3,)), dma((3,)), dma((7,)), dma((7,)), dma((2,)),
        ],
        compiler_params=pltpu.CompilerParams(
            collective_id=0, has_side_effects=True, vmem_limit_bytes=56 * 1024 * 1024
        ),
        cost_estimate=pl.CostEstimate(flops=8_000_000_000, bytes_accessed=12_000_000, transcendentals=0),
    )(query_proj[0], key_proj[0], value_proj[0], filters, w_out, cotangent[0], one, back, two, twiddle)
    output, grad_query, grad_key, grad_value, grad_filter, grad_wout = outs
    return (
        output[None],
        grad_query[None],
        grad_key[None],
        grad_value[None],
        grad_filter,
        grad_wout,
    )


def solution(mesh):
    stream = P("dp", "ctx", "tp")
    taps = P("tp", "ctx")
    return jax.shard_map(
        local,
        mesh=mesh,
        in_specs=(stream, stream, stream, taps, P("tp", None), stream),
        out_specs=(stream, stream, stream, stream, taps, taps),
        check_vma=False,
    )
```

```python
import functools
import math

import jax
import jax.numpy as jnp
import ml_dtypes
import numpy as np
from jax import lax
from jax.experimental import pallas as pl
from jax.experimental.pallas import tpu as pltpu
from jax.sharding import PartitionSpec as P

MESH = pl.DeviceIdType.MESH
F32 = jnp.float32
BF16 = jnp.bfloat16

DP = 2
SEQ = 32
ZN = 8
YN = 4
GROUP = DP * SEQ
CH = 8
BLOCKS = 64
LANES = 128
LENGTH = BLOCKS * LANES
ROWS = BLOCKS * CH
STEP = 256


def halves(table):
    high = table.astype(ml_dtypes.bfloat16)
    low = (table - high.astype(np.float64)).astype(ml_dtypes.bfloat16)
    return np.stack([high, low])


@functools.lru_cache(maxsize=None)
def tables():
    k1 = np.arange(BLOCKS)[:, None].astype(np.float64)
    turn = 2 * math.pi * k1 + math.pi / 2
    outer = turn * np.arange(BLOCKS)[None, :] / BLOCKS
    eye = np.eye(CH)
    stage_one = np.concatenate([np.kron(np.cos(outer), eye), np.kron(-np.sin(outer), eye)], axis=0)
    angle = np.repeat(turn * np.arange(LANES)[None, :] / LENGTH, CH, axis=0)
    twiddle = np.stack([np.cos(angle), -np.sin(angle)]).astype(np.float32)
    lane = np.arange(LANES)
    inner = 2 * math.pi * ((lane[:, None] * lane[None, :]) % LANES) / LANES
    c, s = np.cos(inner), np.sin(inner)
    stage_two = np.block([[c, -s], [s, c]])
    stage_two_back = np.block([[c, s], [-s, c]])
    return (
        halves(stage_one),
        halves(stage_one.T),
        np.concatenate([halves(stage_two), halves(stage_two_back)]),
        twiddle,
    )


def dot(a, b):
    return jnp.dot(a, b, preferred_element_type=F32)


def split(x):
    high = x.astype(BF16)
    return high, (x - high.astype(F32)).astype(BF16)


def kernel(
    factor,
    q_hbm, k_hbm, v_hbm, f_hbm, w_hbm, cot_hbm, one_hbm, back_hbm, two_hbm, tw_hbm,
    out_hbm, gq_hbm, gk_hbm, gv_hbm, gf_hbm, gw_hbm,
    q_ref, k_ref, v_ref, f_ref, w_ref,
    out_ref, gq_ref, gk_ref, gv_ref, gf_ref, gw_ref,
    one, back, two, tw,
    mix_send, mix_recv, fil_send, fil_recv, gc_send, gc_recv,
    conv_send, conv_recv, gm_send, gm_recv, fg_send, fg_recv, fg_part,
    cot_all, cot_t, cot_p, gg, xcat, spec_m, spec_f, spec_g, v_hi, v_lo,
    gated, gated_p, w_send, w_recv, z_send, z_recv, d_send, d_recv,
    core_send, core_recv, x_send, x_recv, own,
    load_sem, store_sem, send_sem, recv_sem, tp_send, tp_recv, dp_send, dp_recv,
    y_ssem, y_rsem, z_ssem, z_rsem,
):
    d = lax.axis_index("dp")
    j = lax.axis_index("ctx")
    t = lax.axis_index("tp")
    z = j // YN
    y = lax.rem(j, YN)
    core = lax.rem(t, 2)
    hi_x = t // 2
    me = d * SEQ + j
    t_core = hi_x * 2 + (1 - core)
    t_x = (1 - hi_x) * 2 + core
    t_far = (1 - hi_x) * 2 + (1 - core)

    def peer(offset):
        p = lax.rem(me + offset, GROUP)
        return p, {"dp": p // SEQ, "ctx": lax.rem(p, SEQ)}

    barrier = pltpu.get_barrier_semaphore()

    def greet(i, carry):
        pl.semaphore_signal(barrier, inc=1, device_id=peer(i)[1], device_id_type=MESH)
        return carry

    def load(src, dst, index):
        copy = pltpu.make_async_copy(src, dst, load_sem.at[index])
        copy.start()
        return copy

    def store(src, dst, index):
        copy = pltpu.make_async_copy(src, dst, store_sem.at[index])
        copy.start()
        return copy

    load_f = load(f_hbm, f_ref, 0)
    load_k = load(k_hbm, k_ref, 1)
    load_v = load(v_hbm, v_ref, 2)
    load_cot = load(cot_hbm, cot_all.at[t], 3)
    lax.fori_loop(1, GROUP, greet, 0)
    for other in (t_core, t_x):
        pl.semaphore_signal(barrier, inc=1, device_id={"tp": other}, device_id_type=MESH)
    load_w = load(w_hbm, w_ref, 4)
    load_q = load(q_hbm, q_ref, 5)
    load_tables = [
        load(src, dst, 6 + i)
        for i, (src, dst) in enumerate(((one_hbm, one), (two_hbm, two), (tw_hbm, tw), (back_hbm, back)))
    ]

    def to_chunks(rows):
        count = rows.shape[0] // CH
        parts = [rows[:, h * LANES : (h + 1) * LANES].reshape(count, CH, LANES) for h in range(2)]
        return jnp.concatenate(parts, axis=1).astype(BF16)

    def from_chunks(ref):
        chunks = ref[...].astype(F32)
        count = chunks.shape[0]
        parts = [chunks[:, h * CH : (h + 1) * CH, :].reshape(count * CH, LANES) for h in range(2)]
        return jnp.concatenate(parts, axis=1)

    half = SEQ * CH
    load_f.wait()
    fil_send[...] = to_chunks(f_ref[pl.ds(pl.multiple_of(d * half, half), half), :])
    fil_recv[j] = fil_send[j]
    load_k.wait()
    load_v.wait()
    mix_send[...] = to_chunks((k_ref[...].astype(F32) * v_ref[...].astype(F32)).T)
    mix_recv[me] = mix_send[me]
    load_cot.wait()

    pl.semaphore_wait(barrier, GROUP + 1)

    def remote(src, dst, ssem, rsem, device):
        return pltpu.make_async_remote_copy(
            src_ref=src, dst_ref=dst, send_sem=ssem, recv_sem=rsem, device_id=device, device_id_type=MESH
        )

    def tp_copy(src, dst, index, to):
        return remote(src, dst, tp_send.at[index], tp_recv.at[index], {"tp": to})

    def dp_copy(src, dst, index):
        return remote(src, dst, dp_send.at[index], dp_recv.at[index], {"dp": 1 - d})

    cot_core = tp_copy(cot_all.at[t], cot_all.at[t], 0, t_core)
    cot_x = tp_copy(cot_all.at[t], cot_all.at[t], 1, t_x)
    cot_x.start()
    cot_core.start()

    def scatter(src, dst, index, first=1, last=GROUP):
        def start(i, carry):
            p, device = peer(i)
            remote(src.at[p], dst.at[me], send_sem.at[index], recv_sem.at[index], device).start()
            return carry

        lax.fori_loop(first, last, start, 0)

    def scatter_same(src, dst, index):
        def start(i, carry):
            p = lax.rem(j + i, SEQ)
            remote(src.at[p], dst.at[j], send_sem.at[index], recv_sem.at[index], {"ctx": p}).start()
            return carry

        lax.fori_loop(1, SEQ, start, 0)

    def whole(ref, index):
        part = ref.at[pl.ds(0, ref.shape[0] - 1)]
        return remote(part, part, send_sem.at[index], recv_sem.at[index], {"tp": t_core})

    scatter_same(fil_send, fil_recv, 1)
    scatter(mix_send, mix_recv, 0)

    width = q_ref.shape[1]
    positions = q_ref.shape[0]
    half_rows = cot_t.shape[2]

    def grad_part(o):
        weights = w_ref[:, pl.ds(pl.multiple_of(o * width, width), width)]
        return lax.dot_general(
            cot_all[o], weights, (((1,), (1,)), ((), ())), preferred_element_type=F32
        )

    per = width // (DP * half_rows)

    def turn(o):
        turned = cot_all[o].astype(F32).T.astype(BF16)
        cot_t[pl.ds(o * per, per)] = turned.reshape(per, DP, half_rows, positions)

    def rows_of(i, base=0):
        return pl.ds(pl.multiple_of(base + i * STEP, STEP), STEP)

    def forward_transform(recv, count, spec):
        for b in range(count):
            xcat[:, b * LANES : (b + 1) * LANES] = recv[b * SEQ : (b + 1) * SEQ].reshape(ROWS, LANES)

        def body(i, carry):
            x = xcat[:, : count * LANES]
            real = dot(one[0, rows_of(i), :], x) + dot(one[1, rows_of(i), :], x)
            imag = dot(one[0, rows_of(i, ROWS), :], x) + dot(one[1, rows_of(i, ROWS), :], x)
            c, s = tw[0, rows_of(i), :], tw[1, rows_of(i), :]
            for b in range(count):
                re = real[:, b * LANES : (b + 1) * LANES]
                im = imag[:, b * LANES : (b + 1) * LANES]
                high, low = split(jnp.concatenate([re * c - im * s, re * s + im * c], axis=1))
                spec[b, rows_of(i), :] = dot(high, two[0]) + dot(low, two[0]) + dot(high, two[1])
            return carry

        lax.fori_loop(0, ROWS // STEP, body, 0)

    def inverse_transform(product, count, send):
        def first(i, carry):
            c, s = tw[0, rows_of(i), :], tw[1, rows_of(i), :]
            for b in range(count):
                high, low = split(jnp.concatenate(product(b, rows_of(i)), axis=1))
                u = dot(high, two[2]) + dot(low, two[2]) + dot(high, two[3])
                re, im = u[:, :LANES], u[:, LANES:]
                lanes = slice(b * LANES, (b + 1) * LANES)
                high, low = split(re * c + im * s)
                v_hi[rows_of(i), lanes] = high
                v_lo[rows_of(i), lanes] = low
                high, low = split(im * c - re * s)
                v_hi[rows_of(i, ROWS), lanes] = high
                v_lo[rows_of(i, ROWS), lanes] = low
            return carry

        lax.fori_loop(0, ROWS // STEP, first, 0)

        def second(i, carry):
            high, low = v_hi[:, : count * LANES], v_lo[:, : count * LANES]
            table = back[0, rows_of(i), :]
            result = dot(table, high) + dot(table, low) + dot(back[1, rows_of(i), :], high)
            result = (result * (1.0 / LENGTH)).astype(BF16)
            chunks = STEP // (2 * CH)
            for b in range(count):
                part = result[:, b * LANES : (b + 1) * LANES].reshape(chunks, 2 * CH, LANES)
                send[pl.ds(b * SEQ + i * chunks, chunks)] = part
            return carry

        lax.fori_loop(0, ROWS // STEP, second, 0)

    def pair(ref, b, rows):
        return ref[b, rows, :LANES], ref[b, rows, LANES:]

    def conv_product(b, rows):
        fr, fi = pair(spec_f, 0, rows)
        mr, mi = pair(spec_m, b, rows)
        return fr * mr - fi * mi, fr * mi + fi * mr

    def grad_product(b, rows):
        fr, fi = pair(spec_f, 0, rows)
        gr, gi = pair(spec_g, b, rows)
        return fr * gr + fi * gi, fr * gi - fi * gr

    def taps_product(_, rows):
        real, imag = 0.0, 0.0
        for b in range(DP):
            mr, mi = pair(spec_m, b, rows)
            gr, gi = pair(spec_g, b, rows)
            real += gr * mr + gi * mi
            imag += gi * mr - gr * mi
        return real, imag

    load_w.wait()
    gg[...] = grad_part(t)
    turn(t)
    cot_core.wait_recv()
    gg[...] += grad_part(t_core)
    turn(t_core)
    for copy in load_tables:
        copy.wait()
    whole(fil_recv, 1).wait_recv()
    forward_transform(fil_recv, 1, spec_f)
    cot_x.wait_recv()
    forward = tp_copy(cot_all.at[t_x], cot_all.at[t_x], 2, t_core)
    forward.start()
    gg[...] += grad_part(t_x)
    load_q.wait()
    forward.wait_recv()
    total = gg[...] + grad_part(t_far)
    gg[...] = total
    gc_send[...] = to_chunks((total * q_ref[...].astype(F32)).T)
    gc_recv[me] = gc_send[me]
    scatter(gc_send, gc_recv, 2, 1, GROUP // 2)
    turn(t_x)
    turn(t_far)
    cot_pair = dp_copy(cot_t.at[:, 1 - d], cot_p, 0)
    cot_pair.start()

    whole(mix_recv, 0).wait_recv()
    forward_transform(mix_recv, DP, spec_m)
    inverse_transform(conv_product, DP, conv_send)
    conv_recv[me] = conv_send[me]
    scatter(conv_send, conv_recv, 3)
    scatter(gc_send, gc_recv, 2, GROUP // 2, GROUP)

    whole(conv_recv, 3).wait_recv()
    conv = from_chunks(conv_recv).T
    gated[...] = (q_ref[...].astype(F32) * conv).astype(BF16)
    gated_pair = dp_copy(gated, gated_p, 1)
    gated_pair.start()
    gq_ref[...] = (gg[...] * conv).astype(BF16)
    stores = [store(gq_ref, gq_hbm, 1)]

    def partial(o):
        return dot(gated[...], w_ref[:, pl.ds(pl.multiple_of(o * width, width), width)])

    core_send[0] = partial(t_far)
    core_send[1] = partial(t_core)
    core_copy = tp_copy(core_send, core_recv, 3, t_core)
    core_copy.start()

    whole(gc_recv, 2).wait_recv()
    forward_transform(gc_recv, DP, spec_g)
    inverse_transform(grad_product, DP, gm_send)
    gm_recv[me] = gm_send[me]
    scatter(gm_send, gm_recv, 4)
    inverse_transform(taps_product, 1, fg_send)
    fg_recv[j] = fg_send[j]
    scatter_same(fg_send, fg_recv, 5)

    cot_pair.wait_recv()
    gated_pair.wait_recv()
    chunks = w_send.shape[0]
    lanes = width // chunks
    planes = ZN // 2
    y_copies = []
    for c in range(chunks):
        cols = slice(c * lanes, (c + 1) * lanes)

        def weight(i, carry, c=c, cols=cols):
            blocks = pl.ds(i * planes * YN, planes * YN)
            mine = cot_t[blocks, d].reshape(planes * YN * half_rows, positions)
            other = cot_p[blocks].reshape(planes * YN * half_rows, positions)
            term = dot(mine, gated[:, cols]) + dot(other, gated_p[:, cols])
            term = term.astype(BF16).reshape(planes, YN, half_rows, lanes)
            for to in range(YN):
                w_send[c, to, pl.ds(i * planes, planes)] = term[:, to]
            return carry

        lax.fori_loop(0, 2, weight, 0)
        for step in (2, 1, 3):
            to = lax.rem(y + step, YN)
            copy = remote(
                w_send.at[c, to], w_recv.at[c, step - 1], y_ssem.at[c, step - 1], y_rsem.at[c, step - 1],
                {"ctx": z * YN + to},
            )
            copy.start()
            y_copies.append(copy)

    other_x = partial(t_x)
    own[...] = partial(t)
    core_copy.wait_recv()
    x_send[...] = (other_x + core_recv[0]).astype(BF16)
    x_copy = tp_copy(x_send, x_recv, 4, t_x)
    x_copy.start()

    z_copies = []

    def reduce_y(c):
        for copy in y_copies[c * 3 : c * 3 + 3]:
            copy.wait_recv()
        value = w_send[c, y].astype(F32)
        for slot in range(YN - 1):
            value += w_recv[c, slot].astype(F32)
        z_send[c] = value.astype(BF16)
        z_recv[c, z] = z_send[c, z]
        for step in (4, 3, 5, 2, 6, 1, 7):
            to = lax.rem(z + step, ZN)
            copy = remote(
                z_send.at[c, to], z_recv.at[c, z], z_ssem.at[c, step - 1], z_rsem.at[c, step - 1],
                {"ctx": to * YN + y},
            )
            copy.start()
            z_copies.append(copy)

    reduce_y(0)
    whole(gm_recv, 4).wait_recv()
    grad_mixed = from_chunks(gm_recv).T
    gk_ref[...] = (grad_mixed * v_ref[...].astype(F32)).astype(BF16)
    gv_ref[...] = (grad_mixed * k_ref[...].astype(F32)).astype(BF16)
    stores += [store(gk_ref, gk_hbm, 2), store(gv_ref, gv_hbm, 3)]
    whole(fg_recv, 5).wait_recv()
    fg_pair = dp_copy(fg_recv, fg_part, 2)
    fg_pair.start()
    for c in range(1, chunks):
        reduce_y(c)
    x_copy.wait_recv()
    out_ref[...] = (own[...] + core_recv[1] + x_recv[...].astype(F32)).astype(BF16)
    stores.append(store(out_ref, out_hbm, 0))
    gf_ref[pl.ds(pl.multiple_of(d * half, half), half), :] = from_chunks(fg_recv) * factor
    fg_pair.wait_recv()
    gf_ref[pl.ds(pl.multiple_of((1 - d) * half, half), half), :] = from_chunks(fg_part) * factor
    stores.append(store(gf_ref, gf_hbm, 4))

    for c in range(chunks):
        for copy in z_copies[c * (ZN - 1) : (c + 1) * (ZN - 1)]:
            copy.wait_recv()
        value = z_recv[c, 0].astype(F32)
        for slot in range(1, ZN):
            value += z_recv[c, slot].astype(F32)
        d_send[:, c * lanes : (c + 1) * lanes] = value * factor
    d_copy = dp_copy(d_send, d_recv, 3)
    d_copy.start()
    gw_ref[pl.ds(pl.multiple_of(d * half_rows, half_rows), half_rows), :] = d_send[...]
    d_copy.wait_recv()
    gw_ref[pl.ds(pl.multiple_of((1 - d) * half_rows, half_rows), half_rows), :] = d_recv[...]
    stores.append(store(gw_ref, gw_hbm, 5))

    for copy in (cot_core, cot_x, forward, core_copy, x_copy, cot_pair, gated_pair, fg_pair, d_copy):
        copy.wait_send()
    for copy in y_copies + z_copies:
        copy.wait_send()
    for index, ref in enumerate((mix_send, fil_send, gc_send, conv_send, gm_send, fg_send)):
        whole(ref, index).wait_send()
    for copy in stores:
        copy.wait()


def hand_over(*refs):
    count = (len(refs) - 2) // 3
    sources, targets, buffers = refs[:count], refs[count : 2 * count], refs[2 * count : 3 * count]
    in_sem, out_sem = refs[3 * count :]
    loads = [pltpu.make_async_copy(sources[i], buffers[i], in_sem.at[i]) for i in range(count)]
    stores = [pltpu.make_async_copy(buffers[i], targets[i], out_sem.at[i]) for i in range(count)]
    for copy in loads:
        copy.start()
    for load, store in zip(loads, stores):
        load.wait()
        store.start()
    for copy in stores:
        copy.wait()


def local(query_proj, key_proj, value_proj, filters, w_out, cotangent):
    positions, channels = query_proj.shape[1:]
    features = w_out.shape[1] // SEQ
    half_rows = features // DP
    factor = 1.0 / math.sqrt(DP * LENGTH)
    one, back, two, twiddle = (jnp.asarray(table) for table in tables())
    stream = jax.ShapeDtypeStruct((positions, channels), BF16)
    anywhere = pl.BlockSpec(memory_space=pl.ANY)
    chunks = pltpu.VMEM((GROUP, 2 * CH, LANES), BF16)
    half_chunks = pltpu.VMEM((SEQ, 2 * CH, LANES), BF16)
    stream_buffer = pltpu.VMEM((positions, channels), BF16)
    wide_buffer = pltpu.VMEM((positions, channels), F32)
    cut = 2
    lanes = channels // cut
    dma = pltpu.SemaphoreType.DMA
    out_shape = (
        stream,
        stream,
        stream,
        stream,
        jax.ShapeDtypeStruct((channels, positions), F32),
        jax.ShapeDtypeStruct((features, channels), F32),
    )
    outs = pl.pallas_call(
        functools.partial(kernel, factor),
        out_shape=out_shape,
        in_specs=[anywhere] * 10,
        out_specs=[anywhere] * 6,
        scratch_shapes=[
            stream_buffer, stream_buffer, stream_buffer,
            pltpu.VMEM(filters.shape, F32),
            pltpu.VMEM(w_out.shape, BF16),
            *[pltpu.VMEM(out.shape, out.dtype) for out in out_shape],
            pltpu.VMEM(one.shape, BF16),
            pltpu.VMEM(back.shape, BF16),
            pltpu.VMEM(two.shape, BF16),
            pltpu.VMEM(twiddle.shape, F32),
            chunks, chunks, half_chunks, half_chunks, chunks, chunks,
            chunks, chunks, chunks, chunks, half_chunks, half_chunks, half_chunks,
            pltpu.VMEM((4, positions, channels), BF16),
            pltpu.VMEM((SEQ, DP, half_rows, positions), BF16),
            pltpu.VMEM((SEQ, half_rows, positions), BF16),
            wide_buffer,
            pltpu.VMEM((ROWS, DP * LANES), BF16),
            pltpu.VMEM((DP, ROWS, 2 * LANES), F32),
            pltpu.VMEM((1, ROWS, 2 * LANES), F32),
            pltpu.VMEM((DP, ROWS, 2 * LANES), F32),
            pltpu.VMEM((2 * ROWS, DP * LANES), BF16),
            pltpu.VMEM((2 * ROWS, DP * LANES), BF16),
            stream_buffer, stream_buffer,
            pltpu.VMEM((cut, YN, ZN, half_rows, lanes), BF16),
            pltpu.VMEM((cut, YN - 1, ZN, half_rows, lanes), BF16),
            pltpu.VMEM((cut, ZN, half_rows, lanes), BF16),
            pltpu.VMEM((cut, ZN, half_rows, lanes), BF16),
            pltpu.VMEM((half_rows, channels), F32),
            pltpu.VMEM((half_rows, channels), F32),
            pltpu.VMEM((2, positions, channels), F32),
            pltpu.VMEM((2, positions, channels), F32),
            stream_buffer, stream_buffer,
            wide_buffer,
            dma((10,)), dma((6,)), dma((6,)), dma((6,)), dma((5,)), dma((5,)), dma((4,)), dma((4,)),
            dma((cut, 3)), dma((cut, 3)), dma((cut, 7)), dma((cut, 7)),
        ],
        compiler_params=pltpu.CompilerParams(
            collective_id=0, has_side_effects=True, vmem_limit_bytes=56 * 1024 * 1024
        ),
        cost_estimate=pl.CostEstimate(flops=8_000_000_000, bytes_accessed=12_000_000, transcendentals=0),
    )(query_proj[0], key_proj[0], value_proj[0], filters, w_out, cotangent[0], one, back, two, twiddle)
    outs = pl.pallas_call(
        hand_over,
        out_shape=out_shape,
        in_specs=[anywhere] * 6,
        out_specs=[anywhere] * 6,
        scratch_shapes=[*[pltpu.VMEM(out.shape, out.dtype) for out in out_shape], dma((6,)), dma((6,))],
    )(*outs)
    output, grad_query, grad_key, grad_value, grad_filter, grad_wout = outs
    return (
        output[None],
        grad_query[None],
        grad_key[None],
        grad_value[None],
        grad_filter,
        grad_wout.T,
    )


def solution(mesh):
    stream = P("dp", "ctx", "tp")
    taps = P("tp", "ctx")
    return jax.shard_map(
        local,
        mesh=mesh,
        in_specs=(stream, stream, stream, taps, P("tp", None), stream),
        out_specs=(stream, stream, stream, stream, taps, taps),
        check_vma=False,
    )
```

```python
import functools
import math

import jax
import jax.numpy as jnp
import ml_dtypes
import numpy as np
from jax import lax
from jax.experimental import pallas as pl
from jax.experimental.pallas import tpu as pltpu
from jax.sharding import PartitionSpec as P

MESH = pl.DeviceIdType.MESH
F32 = jnp.float32
BF16 = jnp.bfloat16

DP = 2
SEQ = 32
ZN = 8
YN = 4
GROUP = DP * SEQ
CH = 8
BLOCKS = 64
LANES = 128
LENGTH = BLOCKS * LANES
ROWS = BLOCKS * CH
STEP = 256


def halves(table):
    high = table.astype(ml_dtypes.bfloat16)
    low = (table - high.astype(np.float64)).astype(ml_dtypes.bfloat16)
    return np.stack([high, low])


@functools.lru_cache(maxsize=None)
def tables():
    k1 = np.arange(BLOCKS)[:, None].astype(np.float64)
    turn = 2 * math.pi * k1 + math.pi / 2
    outer = turn * np.arange(BLOCKS)[None, :] / BLOCKS
    eye = np.eye(CH)
    stage_one = np.concatenate([np.kron(np.cos(outer), eye), np.kron(-np.sin(outer), eye)], axis=0)
    angle = np.repeat(turn * np.arange(LANES)[None, :] / LENGTH, CH, axis=0)
    twiddle = np.stack([np.cos(angle), -np.sin(angle)]).astype(np.float32)
    lane = np.arange(LANES)
    inner = 2 * math.pi * ((lane[:, None] * lane[None, :]) % LANES) / LANES
    c, s = np.cos(inner), np.sin(inner)
    stage_two = np.block([[c, -s], [s, c]])
    stage_two_back = np.block([[c, s], [-s, c]])
    return (
        halves(stage_one),
        halves(stage_one.T),
        np.concatenate([halves(stage_two), halves(stage_two_back)]),
        twiddle,
    )


def dot(a, b):
    return jnp.dot(a, b, preferred_element_type=F32)


def split(x):
    high = x.astype(BF16)
    return high, (x - high.astype(F32)).astype(BF16)


def kernel(
    factor,
    q_hbm, k_hbm, v_hbm, f_hbm, w_hbm, cot_hbm, one_hbm, back_hbm, two_hbm, tw_hbm,
    out_hbm, gq_hbm, gk_hbm, gv_hbm, gf_hbm, gw_hbm,
    q_ref, k_ref, v_ref, f_ref, w_ref,
    out_ref, gq_ref, gk_ref, gv_ref, gf_ref, gw_ref,
    one, back, two, tw,
    mix_send, mix_recv, fil_send, fil_recv, gc_send, gc_recv,
    conv_send, conv_recv, gm_send, gm_recv, fg_send, fg_recv, fg_part,
    cot_all, cot_t, cot_p, gg, xcat, spec_m, spec_f, spec_g, v_hi, v_lo,
    gated, gated_p, w_send, w_recv, z_send, z_recv, d_send, d_recv,
    core_send, core_recv, x_send, x_recv, own,
    load_sem, store_sem, send_sem, recv_sem, tp_send, tp_recv, dp_send, dp_recv,
    y_ssem, y_rsem, z_ssem, z_rsem,
):
    d = lax.axis_index("dp")
    j = lax.axis_index("ctx")
    t = lax.axis_index("tp")
    z = j // YN
    y = lax.rem(j, YN)
    core = lax.rem(t, 2)
    hi_x = t // 2
    me = d * SEQ + j
    t_core = hi_x * 2 + (1 - core)
    t_x = (1 - hi_x) * 2 + core
    t_far = (1 - hi_x) * 2 + (1 - core)

    def peer(offset):
        p = lax.rem(me + offset, GROUP)
        return p, {"dp": p // SEQ, "ctx": lax.rem(p, SEQ)}

    barrier = pltpu.get_barrier_semaphore()

    def greet(i, carry):
        pl.semaphore_signal(barrier, inc=1, device_id=peer(i)[1], device_id_type=MESH)
        return carry

    def load(src, dst, index):
        copy = pltpu.make_async_copy(src, dst, load_sem.at[index])
        copy.start()
        return copy

    def store(src, dst, index):
        copy = pltpu.make_async_copy(src, dst, store_sem.at[index])
        copy.start()
        return copy

    lax.fori_loop(1, GROUP, greet, 0, unroll=9)
    for other in (t_core, t_x):
        pl.semaphore_signal(barrier, inc=1, device_id={"tp": other}, device_id_type=MESH)
    load_f = load(f_hbm, f_ref, 0)
    load_cot = load(cot_hbm, cot_all.at[t], 3)
    load_k = load(k_hbm, k_ref, 1)
    load_v = load(v_hbm, v_ref, 2)
    load_w = load(w_hbm, w_ref, 4)
    load_q = load(q_hbm, q_ref, 5)
    load_tables = [
        load(src, dst, 6 + i)
        for i, (src, dst) in enumerate(((one_hbm, one), (two_hbm, two), (tw_hbm, tw), (back_hbm, back)))
    ]

    def to_chunks(rows):
        count = rows.shape[0] // CH
        parts = [rows[:, h * LANES : (h + 1) * LANES].reshape(count, CH, LANES) for h in range(2)]
        return jnp.concatenate(parts, axis=1).astype(BF16)

    def from_chunks(ref):
        chunks = ref[...].astype(F32)
        count = chunks.shape[0]
        parts = [chunks[:, h * CH : (h + 1) * CH, :].reshape(count * CH, LANES) for h in range(2)]
        return jnp.concatenate(parts, axis=1)

    half = SEQ * CH
    load_f.wait()
    fil_send[...] = to_chunks(f_ref[pl.ds(pl.multiple_of(d * half, half), half), :])
    fil_recv[j] = fil_send[j]
    load_cot.wait()

    pl.semaphore_wait(barrier, GROUP + 1)

    def remote(src, dst, ssem, rsem, device):
        return pltpu.make_async_remote_copy(
            src_ref=src, dst_ref=dst, send_sem=ssem, recv_sem=rsem, device_id=device, device_id_type=MESH
        )

    def tp_copy(src, dst, index, to):
        return remote(src, dst, tp_send.at[index], tp_recv.at[index], {"tp": to})

    def dp_copy(src, dst, index):
        return remote(src, dst, dp_send.at[index], dp_recv.at[index], {"dp": 1 - d})

    cot_core = tp_copy(cot_all.at[t], cot_all.at[t], 0, t_core)
    cot_x = tp_copy(cot_all.at[t], cot_all.at[t], 1, t_x)
    cot_x.start()
    cot_core.start()

    def scatter(src, dst, index, first=1, last=GROUP):
        def start(i, carry):
            p, device = peer(i)
            remote(src.at[p], dst.at[me], send_sem.at[index], recv_sem.at[index], device).start()
            return carry

        lax.fori_loop(first, last, start, 0)

    def scatter_same(src, dst, index):
        def start(i, carry):
            p = lax.rem(j + i, SEQ)
            remote(src.at[p], dst.at[j], send_sem.at[index], recv_sem.at[index], {"ctx": p}).start()
            return carry

        lax.fori_loop(1, SEQ, start, 0)

    def whole(ref, index):
        part = ref.at[pl.ds(0, ref.shape[0] - 1)]
        return remote(part, part, send_sem.at[index], recv_sem.at[index], {"tp": t_core})

    scatter_same(fil_send, fil_recv, 1)
    load_k.wait()
    load_v.wait()
    mix_send[...] = to_chunks((k_ref[...].astype(F32) * v_ref[...].astype(F32)).T)
    mix_recv[me] = mix_send[me]
    scatter(mix_send, mix_recv, 0)

    width = q_ref.shape[1]
    positions = q_ref.shape[0]
    half_rows = cot_t.shape[2]

    def grad_part(o):
        weights = w_ref[:, pl.ds(pl.multiple_of(o * width, width), width)]
        return lax.dot_general(
            cot_all[o], weights, (((1,), (1,)), ((), ())), preferred_element_type=F32
        )

    per = width // (DP * half_rows)

    def turn(o):
        turned = cot_all[o].astype(F32).T.astype(BF16)
        cot_t[pl.ds(o * per, per)] = turned.reshape(per, DP, half_rows, positions)

    def rows_of(i, base=0):
        return pl.ds(pl.multiple_of(base + i * STEP, STEP), STEP)

    def forward_transform(recv, count, spec):
        for b in range(count):
            xcat[:, b * LANES : (b + 1) * LANES] = recv[b * SEQ : (b + 1) * SEQ].reshape(ROWS, LANES)

        def body(i, carry):
            x = xcat[:, : count * LANES]
            real = dot(one[0, rows_of(i), :], x) + dot(one[1, rows_of(i), :], x)
            imag = dot(one[0, rows_of(i, ROWS), :], x) + dot(one[1, rows_of(i, ROWS), :], x)
            c, s = tw[0, rows_of(i), :], tw[1, rows_of(i), :]
            for b in range(count):
                re = real[:, b * LANES : (b + 1) * LANES]
                im = imag[:, b * LANES : (b + 1) * LANES]
                high, low = split(jnp.concatenate([re * c - im * s, re * s + im * c], axis=1))
                spec[b, rows_of(i), :] = dot(high, two[0]) + dot(low, two[0]) + dot(high, two[1])
            return carry

        lax.fori_loop(0, ROWS // STEP, body, 0, unroll=True)

    def inverse_transform(product, count, send):
        def first(i, carry):
            c, s = tw[0, rows_of(i), :], tw[1, rows_of(i), :]
            for b in range(count):
                high, low = split(jnp.concatenate(product(b, rows_of(i)), axis=1))
                u = dot(high, two[2]) + dot(low, two[2]) + dot(high, two[3])
                re, im = u[:, :LANES], u[:, LANES:]
                lanes = slice(b * LANES, (b + 1) * LANES)
                high, low = split(re * c + im * s)
                v_hi[rows_of(i), lanes] = high
                v_lo[rows_of(i), lanes] = low
                high, low = split(im * c - re * s)
                v_hi[rows_of(i, ROWS), lanes] = high
                v_lo[rows_of(i, ROWS), lanes] = low
            return carry

        lax.fori_loop(0, ROWS // STEP, first, 0, unroll=True)

        def second(i, carry):
            high, low = v_hi[:, : count * LANES], v_lo[:, : count * LANES]
            table = back[0, rows_of(i), :]
            result = dot(table, high) + dot(table, low) + dot(back[1, rows_of(i), :], high)
            result = (result * (1.0 / LENGTH)).astype(BF16)
            chunks = STEP // (2 * CH)
            for b in range(count):
                part = result[:, b * LANES : (b + 1) * LANES].reshape(chunks, 2 * CH, LANES)
                send[pl.ds(b * SEQ + i * chunks, chunks)] = part
            return carry

        lax.fori_loop(0, ROWS // STEP, second, 0, unroll=True)

    def pair(ref, b, rows):
        return ref[b, rows, :LANES], ref[b, rows, LANES:]

    def conv_product(b, rows):
        fr, fi = pair(spec_f, 0, rows)
        mr, mi = pair(spec_m, b, rows)
        return fr * mr - fi * mi, fr * mi + fi * mr

    def grad_product(b, rows):
        fr, fi = pair(spec_f, 0, rows)
        gr, gi = pair(spec_g, b, rows)
        return fr * gr + fi * gi, fr * gi - fi * gr

    def taps_product(_, rows):
        real, imag = 0.0, 0.0
        for b in range(DP):
            mr, mi = pair(spec_m, b, rows)
            gr, gi = pair(spec_g, b, rows)
            real += gr * mr + gi * mi
            imag += gi * mr - gr * mi
        return real, imag

    load_w.wait()
    gg[...] = grad_part(t)
    turn(t)
    cot_core.wait_recv()
    gg[...] += grad_part(t_core)
    turn(t_core)
    for copy in load_tables:
        copy.wait()
    whole(fil_recv, 1).wait_recv()
    forward_transform(fil_recv, 1, spec_f)
    cot_x.wait_recv()
    forward = tp_copy(cot_all.at[t_x], cot_all.at[t_x], 2, t_core)
    forward.start()

    def cot_pair(x_index, index):
        blocks = pl.ds(x_index * (SEQ // 2), SEQ // 2)
        return dp_copy(cot_t.at[blocks, 1 - d], cot_p.at[blocks], index)

    cot_pairs = [cot_pair(hi_x, 0), cot_pair(1 - hi_x, 1)]
    cot_pairs[0].start()
    gg[...] += grad_part(t_x)
    load_q.wait()
    forward.wait_recv()
    total = gg[...] + grad_part(t_far)
    gg[...] = total
    gc_send[...] = to_chunks((total * q_ref[...].astype(F32)).T)
    gc_recv[me] = gc_send[me]
    scatter(gc_send, gc_recv, 2, 1, GROUP // 2)
    turn(t_x)
    turn(t_far)
    cot_pairs[1].start()

    whole(mix_recv, 0).wait_recv()
    forward_transform(mix_recv, DP, spec_m)
    inverse_transform(conv_product, DP, conv_send)
    conv_recv[me] = conv_send[me]
    scatter(conv_send, conv_recv, 3)
    scatter(gc_send, gc_recv, 2, GROUP // 2, GROUP)

    cut = gated.shape[0]
    lanes = gated.shape[2]
    sources = GROUP // cut
    gated_pairs = [dp_copy(gated.at[c], gated_p.at[c], 2 + c) for c in range(cut)]
    whole(conv_recv, 3).wait_recv()
    for c in range(cut):
        cols = slice(c * lanes, (c + 1) * lanes)
        conv = from_chunks(conv_recv.at[pl.ds(c * sources, sources)]).T
        gated[c] = (q_ref[:, cols].astype(F32) * conv).astype(BF16)
        gated_pairs[c].start()
        gq_ref[:, cols] = (gg[:, cols] * conv).astype(BF16)
    stores = [store(gq_ref, gq_hbm, 1)]

    def partial(o):
        rows = jnp.concatenate([gated[c] for c in range(cut)], axis=1)
        return dot(rows, w_ref[:, pl.ds(pl.multiple_of(o * width, width), width)])

    core_send[0] = partial(t_far)
    core_send[1] = partial(t_core)
    core_copy = tp_copy(core_send, core_recv, 3, t_core)
    core_copy.start()

    for copy in cot_pairs:
        copy.wait_recv()
    planes = ZN // 2
    y_copies = []

    def weights(c):
        gated_pairs[c].wait_recv()

        def weight(i, carry):
            blocks = pl.ds(i * planes * YN, planes * YN)
            mine = cot_t[blocks, d].reshape(planes * YN * half_rows, positions)
            other = cot_p[blocks].reshape(planes * YN * half_rows, positions)
            term = dot(mine, gated[c]) + dot(other, gated_p[c])
            term = term.astype(BF16).reshape(planes, YN, half_rows, lanes)
            for to in range(YN):
                w_send[c, to, pl.ds(i * planes, planes)] = term[:, to]
            return carry

        lax.fori_loop(0, 2, weight, 0)
        for step in (2, 1, 3):
            to = lax.rem(y + step, YN)
            copy = remote(
                w_send.at[c, to], w_recv.at[c, step - 1], y_ssem.at[c, step - 1], y_rsem.at[c, step - 1],
                {"ctx": z * YN + to},
            )
            copy.start()
            y_copies.append(copy)

    for c in range(cut // 2):
        weights(c)
    whole(gc_recv, 2).wait_recv()
    forward_transform(gc_recv, DP, spec_g)
    inverse_transform(grad_product, DP, gm_send)
    gm_recv[me] = gm_send[me]
    scatter(gm_send, gm_recv, 4)
    for c in range(cut // 2, cut):
        weights(c)
    inverse_transform(taps_product, 1, fg_send)
    fg_recv[j] = fg_send[j]
    scatter_same(fg_send, fg_recv, 5)

    other_x = partial(t_x)
    own[...] = partial(t)
    core_copy.wait_recv()
    x_send[...] = (other_x + core_recv[0]).astype(BF16)
    x_copy = tp_copy(x_send, x_recv, 4, t_x)
    x_copy.start()

    z_copies = []

    def reduce_y(c):
        for copy in y_copies[c * 3 : c * 3 + 3]:
            copy.wait_recv()
        value = w_send[c, y].astype(F32)
        for slot in range(YN - 1):
            value += w_recv[c, slot].astype(F32)
        z_send[c] = value.astype(BF16)
        z_recv[c, z] = z_send[c, z]
        for step in (4, 3, 5, 2, 6, 1, 7):
            to = lax.rem(z + step, ZN)
            copy = remote(
                z_send.at[c, to], z_recv.at[c, z], z_ssem.at[c, step - 1], z_rsem.at[c, step - 1],
                {"ctx": to * YN + y},
            )
            copy.start()
            z_copies.append(copy)

    for c in range(cut - 1):
        reduce_y(c)
    whole(gm_recv, 4).wait_recv()
    grad_mixed = from_chunks(gm_recv).T
    gk_ref[...] = (grad_mixed * v_ref[...].astype(F32)).astype(BF16)
    gv_ref[...] = (grad_mixed * k_ref[...].astype(F32)).astype(BF16)
    stores += [store(gk_ref, gk_hbm, 2), store(gv_ref, gv_hbm, 3)]
    reduce_y(cut - 1)
    whole(fg_recv, 5).wait_recv()
    fg_pair = dp_copy(fg_recv, fg_part, 2 + cut)
    fg_pair.start()
    x_copy.wait_recv()
    out_ref[...] = (own[...] + core_recv[1] + x_recv[...].astype(F32)).astype(BF16)
    stores.append(store(out_ref, out_hbm, 0))
    gf_ref[pl.ds(pl.multiple_of(d * half, half), half), :] = from_chunks(fg_recv) * factor

    for c in range(cut):
        for copy in z_copies[c * (ZN - 1) : (c + 1) * (ZN - 1)]:
            copy.wait_recv()
        value = z_recv[c, 0].astype(F32)
        for slot in range(1, ZN):
            value += z_recv[c, slot].astype(F32)
        d_send[:, c * lanes : (c + 1) * lanes] = value * factor
    d_copy = dp_copy(d_send, d_recv, 3 + cut)
    d_copy.start()
    fg_pair.wait_recv()
    gf_ref[pl.ds(pl.multiple_of((1 - d) * half, half), half), :] = from_chunks(fg_part) * factor
    stores.append(store(gf_ref, gf_hbm, 4))
    gw_ref[pl.ds(pl.multiple_of(d * half_rows, half_rows), half_rows), :] = d_send[...]
    d_copy.wait_recv()
    gw_ref[pl.ds(pl.multiple_of((1 - d) * half_rows, half_rows), half_rows), :] = d_recv[...]
    stores.append(store(gw_ref, gw_hbm, 5))

    for copy in (cot_core, cot_x, forward, core_copy, x_copy, fg_pair, d_copy):
        copy.wait_send()
    for copy in cot_pairs + gated_pairs + y_copies + z_copies:
        copy.wait_send()
    for index, ref in enumerate((mix_send, fil_send, gc_send, conv_send, gm_send, fg_send)):
        whole(ref, index).wait_send()
    for copy in stores:
        copy.wait()


def hand_over(*refs):
    count = (len(refs) - 2) // 3
    sources, targets, buffers = refs[:count], refs[count : 2 * count], refs[2 * count : 3 * count]
    in_sem, out_sem = refs[3 * count :]
    loads = [pltpu.make_async_copy(sources[i], buffers[i], in_sem.at[i]) for i in range(count)]
    stores = [pltpu.make_async_copy(buffers[i], targets[i], out_sem.at[i]) for i in range(count)]
    for copy in loads:
        copy.start()
    for load, store in zip(loads, stores):
        load.wait()
        store.start()
    for copy in stores:
        copy.wait()


def local(query_proj, key_proj, value_proj, filters, w_out, cotangent):
    positions, channels = query_proj.shape[1:]
    features = w_out.shape[1] // SEQ
    half_rows = features // DP
    factor = 1.0 / math.sqrt(DP * LENGTH)
    one, back, two, twiddle = (jnp.asarray(table) for table in tables())
    stream = jax.ShapeDtypeStruct((positions, channels), BF16)
    anywhere = pl.BlockSpec(memory_space=pl.ANY)
    chunks = pltpu.VMEM((GROUP, 2 * CH, LANES), BF16)
    half_chunks = pltpu.VMEM((SEQ, 2 * CH, LANES), BF16)
    stream_buffer = pltpu.VMEM((positions, channels), BF16)
    wide_buffer = pltpu.VMEM((positions, channels), F32)
    cut = channels // LANES
    lanes = LANES
    dma = pltpu.SemaphoreType.DMA
    out_shape = (
        stream,
        stream,
        stream,
        stream,
        jax.ShapeDtypeStruct((channels, positions), F32),
        jax.ShapeDtypeStruct((features, channels), F32),
    )
    outs = pl.pallas_call(
        functools.partial(kernel, factor),
        out_shape=out_shape,
        in_specs=[anywhere] * 10,
        out_specs=[anywhere] * 6,
        scratch_shapes=[
            stream_buffer, stream_buffer, stream_buffer,
            pltpu.VMEM(filters.shape, F32),
            pltpu.VMEM(w_out.shape, BF16),
            *[pltpu.VMEM(out.shape, out.dtype) for out in out_shape],
            pltpu.VMEM(one.shape, BF16),
            pltpu.VMEM(back.shape, BF16),
            pltpu.VMEM(two.shape, BF16),
            pltpu.VMEM(twiddle.shape, F32),
            chunks, chunks, half_chunks, half_chunks, chunks, chunks,
            chunks, chunks, chunks, chunks, half_chunks, half_chunks, half_chunks,
            pltpu.VMEM((4, positions, channels), BF16),
            pltpu.VMEM((SEQ, DP, half_rows, positions), BF16),
            pltpu.VMEM((SEQ, half_rows, positions), BF16),
            wide_buffer,
            pltpu.VMEM((ROWS, DP * LANES), BF16),
            pltpu.VMEM((DP, ROWS, 2 * LANES), F32),
            pltpu.VMEM((1, ROWS, 2 * LANES), F32),
            pltpu.VMEM((DP, ROWS, 2 * LANES), F32),
            pltpu.VMEM((2 * ROWS, DP * LANES), BF16),
            pltpu.VMEM((2 * ROWS, DP * LANES), BF16),
            pltpu.VMEM((cut, positions, lanes), BF16),
            pltpu.VMEM((cut, positions, lanes), BF16),
            pltpu.VMEM((cut, YN, ZN, half_rows, lanes), BF16),
            pltpu.VMEM((cut, YN - 1, ZN, half_rows, lanes), BF16),
            pltpu.VMEM((cut, ZN, half_rows, lanes), BF16),
            pltpu.VMEM((cut, ZN, half_rows, lanes), BF16),
            pltpu.VMEM((half_rows, channels), F32),
            pltpu.VMEM((half_rows, channels), F32),
            pltpu.VMEM((2, positions, channels), F32),
            pltpu.VMEM((2, positions, channels), F32),
            stream_buffer, stream_buffer,
            wide_buffer,
            dma((10,)), dma((6,)), dma((6,)), dma((6,)), dma((5,)), dma((5,)), dma((4 + cut,)), dma((4 + cut,)),
            dma((cut, 3)), dma((cut, 3)), dma((cut, 7)), dma((cut, 7)),
        ],
        compiler_params=pltpu.CompilerParams(
            collective_id=0, has_side_effects=True, vmem_limit_bytes=56 * 1024 * 1024
        ),
        cost_estimate=pl.CostEstimate(flops=8_000_000_000, bytes_accessed=12_000_000, transcendentals=0),
    )(query_proj[0], key_proj[0], value_proj[0], filters, w_out, cotangent[0], one, back, two, twiddle)
    outs = pl.pallas_call(
        hand_over,
        out_shape=out_shape,
        in_specs=[anywhere] * 6,
        out_specs=[anywhere] * 6,
        scratch_shapes=[*[pltpu.VMEM(out.shape, out.dtype) for out in out_shape], dma((6,)), dma((6,))],
    )(*outs)
    output, grad_query, grad_key, grad_value, grad_filter, grad_wout = outs
    return (
        output[None],
        grad_query[None],
        grad_key[None],
        grad_value[None],
        grad_filter,
        grad_wout.T,
    )


def solution(mesh):
    stream = P("dp", "ctx", "tp")
    taps = P("tp", "ctx")
    return jax.shard_map(
        local,
        mesh=mesh,
        in_specs=(stream, stream, stream, taps, P("tp", None), stream),
        out_specs=(stream, stream, stream, stream, taps, taps),
        check_vma=False,
    )
```

```python
import functools
import math

import jax
import jax.numpy as jnp
import ml_dtypes
import numpy as np
from jax import lax
from jax.experimental import pallas as pl
from jax.experimental.pallas import tpu as pltpu
from jax.sharding import PartitionSpec as P

MESH = pl.DeviceIdType.MESH
F32 = jnp.float32
BF16 = jnp.bfloat16

DP = 2
SEQ = 32
ZN = 8
YN = 4
GROUP = DP * SEQ
CH = 8
BLOCKS = 64
LANES = 128
LENGTH = BLOCKS * LANES
ROWS = BLOCKS * CH
STEP = 256


def halves(table):
    high = table.astype(ml_dtypes.bfloat16)
    low = (table - high.astype(np.float64)).astype(ml_dtypes.bfloat16)
    return np.stack([high, low])


@functools.lru_cache(maxsize=None)
def tables():
    k1 = np.arange(BLOCKS)[:, None].astype(np.float64)
    turn = 2 * math.pi * k1 + math.pi / 2
    outer = turn * np.arange(BLOCKS)[None, :] / BLOCKS
    eye = np.eye(CH)
    stage_one = np.concatenate([np.kron(np.cos(outer), eye), np.kron(-np.sin(outer), eye)], axis=0)
    angle = np.repeat(turn * np.arange(LANES)[None, :] / LENGTH, CH, axis=0)
    twiddle = np.stack([np.cos(angle), -np.sin(angle)]).astype(np.float32)
    lane = np.arange(LANES)
    inner = 2 * math.pi * ((lane[:, None] * lane[None, :]) % LANES) / LANES
    c, s = np.cos(inner), np.sin(inner)
    stage_two = np.block([[c, -s], [s, c]])
    stage_two_back = np.block([[c, s], [-s, c]])
    return (
        halves(stage_one),
        halves(stage_one.T),
        np.concatenate([halves(stage_two), halves(stage_two_back)]),
        twiddle,
    )


def dot(a, b):
    return jnp.dot(a, b, preferred_element_type=F32)


def split(x):
    high = x.astype(BF16)
    return high, (x - high.astype(F32)).astype(BF16)


def kernel(
    factor,
    q_hbm, k_hbm, v_hbm, f_hbm, w_hbm, cot_hbm, one_hbm, back_hbm, two_hbm, tw_hbm,
    out_hbm, gq_hbm, gk_hbm, gv_hbm, gf_hbm, gw_hbm,
    q_ref, k_ref, v_ref, f_ref, w_ref,
    out_ref, gq_ref, gk_ref, gv_ref, gf_ref, gw_ref,
    one, back, two, tw,
    mix_send, mix_recv, fil_send, fil_recv, gc_send, gc_recv,
    conv_send, conv_recv, gm_send, gm_recv, fg_send, fg_recv, fg_part,
    cot_all, cot_t, cot_p, gg, xcat, spec_m, spec_f, spec_g, v_hi, v_lo,
    gated, gated_p, w_send, w_recv, z_send, z_recv, first_recv, last_send, last_recv, d_send, d_recv,
    core_send, core_recv, x_send, x_recv, own, across,
    load_sem, store_sem, send_sem, recv_sem, tp_send, tp_recv, dp_send, dp_recv,
    y_ssem, y_rsem, z_ssem, z_rsem,
):
    d = lax.axis_index("dp")
    j = lax.axis_index("ctx")
    t = lax.axis_index("tp")
    z = j // YN
    y = lax.rem(j, YN)
    core = lax.rem(t, 2)
    hi_x = t // 2
    me = d * SEQ + j
    t_core = hi_x * 2 + (1 - core)
    t_x = (1 - hi_x) * 2 + core
    t_far = (1 - hi_x) * 2 + (1 - core)

    def peer(offset):
        p = lax.rem(me + offset, GROUP)
        return p, {"dp": p // SEQ, "ctx": lax.rem(p, SEQ)}

    barrier = pltpu.get_barrier_semaphore()

    def greet(i, carry):
        pl.semaphore_signal(barrier, inc=1, device_id=peer(i)[1], device_id_type=MESH)
        return carry

    def load(src, dst, index):
        copy = pltpu.make_async_copy(src, dst, load_sem.at[index])
        copy.start()
        return copy

    def store(src, dst, index):
        copy = pltpu.make_async_copy(src, dst, store_sem.at[index])
        copy.start()
        return copy

    lax.fori_loop(1, GROUP, greet, 0, unroll=9)
    for other in (t_core, t_x):
        pl.semaphore_signal(barrier, inc=1, device_id={"tp": other}, device_id_type=MESH)
    load_f = load(f_hbm, f_ref, 0)
    load_cot = load(cot_hbm, cot_all.at[t], 3)
    load_k = load(k_hbm, k_ref, 1)
    load_v = load(v_hbm, v_ref, 2)
    load_w = load(w_hbm, w_ref, 4)
    load_q = load(q_hbm, q_ref, 5)
    load_tables = [
        load(src, dst, 6 + i)
        for i, (src, dst) in enumerate(((one_hbm, one), (two_hbm, two), (tw_hbm, tw), (back_hbm, back)))
    ]

    def to_chunks(rows):
        count = rows.shape[0] // CH
        parts = [rows[:, h * LANES : (h + 1) * LANES].reshape(count, CH, LANES) for h in range(2)]
        return jnp.concatenate(parts, axis=1).astype(BF16)

    def from_chunks(ref):
        chunks = ref[...].astype(F32)
        count = chunks.shape[0]
        parts = [chunks[:, h * CH : (h + 1) * CH, :].reshape(count * CH, LANES) for h in range(2)]
        return jnp.concatenate(parts, axis=1)

    half = SEQ * CH
    load_f.wait()
    fil_send[...] = to_chunks(f_ref[pl.ds(pl.multiple_of(d * half, half), half), :])
    fil_recv[j] = fil_send[j]
    load_cot.wait()

    pl.semaphore_wait(barrier, GROUP + 1)

    def remote(src, dst, ssem, rsem, device):
        return pltpu.make_async_remote_copy(
            src_ref=src, dst_ref=dst, send_sem=ssem, recv_sem=rsem, device_id=device, device_id_type=MESH
        )

    def tp_copy(src, dst, index, to):
        return remote(src, dst, tp_send.at[index], tp_recv.at[index], {"tp": to})

    def dp_copy(src, dst, index):
        return remote(src, dst, dp_send.at[index], dp_recv.at[index], {"dp": 1 - d})

    cot_core = tp_copy(cot_all.at[t], cot_all.at[t], 0, t_core)
    cot_x = tp_copy(cot_all.at[t], cot_all.at[t], 1, t_x)
    cot_x.start()
    cot_core.start()

    def scatter(src, dst, index, first=1, last=GROUP):
        def start(i, carry):
            p, device = peer(i)
            remote(src.at[p], dst.at[me], send_sem.at[index], recv_sem.at[index], device).start()
            return carry

        lax.fori_loop(first, last, start, 0)

    def scatter_same(src, dst, index):
        def start(i, carry):
            p = lax.rem(j + i, SEQ)
            remote(src.at[p], dst.at[j], send_sem.at[index], recv_sem.at[index], {"ctx": p}).start()
            return carry

        lax.fori_loop(1, SEQ, start, 0)

    def whole(ref, index):
        part = ref.at[pl.ds(0, ref.shape[0] - 1)]
        return remote(part, part, send_sem.at[index], recv_sem.at[index], {"tp": t_core})

    scatter_same(fil_send, fil_recv, 1)
    load_k.wait()
    load_v.wait()
    mix_send[...] = to_chunks((k_ref[...].astype(F32) * v_ref[...].astype(F32)).T)
    mix_recv[me] = mix_send[me]
    scatter(mix_send, mix_recv, 0)

    width = q_ref.shape[1]
    positions = q_ref.shape[0]
    half_rows = cot_t.shape[2]

    def grad_part(o):
        weights = w_ref[:, pl.ds(pl.multiple_of(o * width, width), width)]
        return lax.dot_general(
            cot_all[o], weights, (((1,), (1,)), ((), ())), preferred_element_type=F32
        )

    per = width // (DP * half_rows)

    def turn(o):
        turned = cot_all[o].astype(F32).T.astype(BF16)
        cot_t[pl.ds(o * per, per)] = turned.reshape(per, DP, half_rows, positions)

    def rows_of(i, base=0):
        return pl.ds(pl.multiple_of(base + i * STEP, STEP), STEP)

    def forward_transform(recv, count, spec, fine=True):
        for b in range(count):
            xcat[:, b * LANES : (b + 1) * LANES] = recv[b * SEQ : (b + 1) * SEQ].reshape(ROWS, LANES)

        def body(i, carry):
            x = xcat[:, : count * LANES]
            real = dot(one[0, rows_of(i), :], x)
            imag = dot(one[0, rows_of(i, ROWS), :], x)
            if fine:
                real += dot(one[1, rows_of(i), :], x)
                imag += dot(one[1, rows_of(i, ROWS), :], x)
            c, s = tw[0, rows_of(i), :], tw[1, rows_of(i), :]
            for b in range(count):
                re = real[:, b * LANES : (b + 1) * LANES]
                im = imag[:, b * LANES : (b + 1) * LANES]
                high, low = split(jnp.concatenate([re * c - im * s, re * s + im * c], axis=1))
                spec[b, rows_of(i), :] = dot(high, two[0]) + dot(low, two[0]) + dot(high, two[1])
            return carry

        lax.fori_loop(0, ROWS // STEP, body, 0, unroll=True)

    def inverse_transform(product, count, send, fine=True, sent=None):
        def first(i, carry):
            c, s = tw[0, rows_of(i), :], tw[1, rows_of(i), :]
            for b in range(count):
                high, low = split(jnp.concatenate(product(b, rows_of(i)), axis=1))
                u = dot(high, two[2]) + dot(low, two[2]) + dot(high, two[3])
                re, im = u[:, :LANES], u[:, LANES:]
                lanes = slice(b * LANES, (b + 1) * LANES)
                high, low = split(re * c + im * s)
                v_hi[rows_of(i), lanes] = high
                v_lo[rows_of(i), lanes] = low
                high, low = split(im * c - re * s)
                v_hi[rows_of(i, ROWS), lanes] = high
                v_lo[rows_of(i, ROWS), lanes] = low
            return carry

        lax.fori_loop(0, ROWS // STEP, first, 0, unroll=True)

        chunks = STEP // (2 * CH)
        for i in range(ROWS // STEP):
            high, low = v_hi[:, : count * LANES], v_lo[:, : count * LANES]
            table = back[0, rows_of(i), :]
            result = dot(table, high) + dot(table, low)
            if fine:
                result += dot(back[1, rows_of(i), :], high)
            result = (result * (1.0 / LENGTH)).astype(BF16)
            for b in range(count):
                part = result[:, b * LANES : (b + 1) * LANES].reshape(chunks, 2 * CH, LANES)
                send[pl.ds(b * SEQ + i * chunks, chunks)] = part
            if sent is not None:
                sent(i * chunks, chunks)

    def scatter_part(src, dst, index):
        def part(base, length):
            def start(i, carry):
                sequence = lax.rem(d + 1 + i // length, DP)
                position = base + lax.rem(i + j, length)
                p = sequence * SEQ + position

                @pl.when(p != me)
                def _():
                    device = {"dp": sequence, "ctx": position}
                    remote(src.at[p], dst.at[me], send_sem.at[index], recv_sem.at[index], device).start()

                return carry

            lax.fori_loop(0, DP * length, start, 0)

        return part

    def pair(ref, b, rows):
        return ref[b, rows, :LANES], ref[b, rows, LANES:]

    def conv_product(b, rows):
        fr, fi = pair(spec_f, 0, rows)
        mr, mi = pair(spec_m, b, rows)
        return fr * mr - fi * mi, fr * mi + fi * mr

    def grad_product(b, rows):
        fr, fi = pair(spec_f, 0, rows)
        gr, gi = pair(spec_g, b, rows)
        return fr * gr + fi * gi, fr * gi - fi * gr

    def taps_product(_, rows):
        real, imag = 0.0, 0.0
        for b in range(DP):
            mr, mi = pair(spec_m, b, rows)
            gr, gi = pair(spec_g, b, rows)
            real += gr * mr + gi * mi
            imag += gi * mr - gr * mi
        return real, imag

    load_w.wait()
    gg[...] = grad_part(t)
    turn(t)
    cot_core.wait_recv()
    gg[...] += grad_part(t_core)
    turn(t_core)
    for copy in load_tables:
        copy.wait()
    whole(fil_recv, 1).wait_recv()
    forward_transform(fil_recv, 1, spec_f)
    cot_x.wait_recv()
    forward = tp_copy(cot_all.at[t_x], cot_all.at[t_x], 2, t_core)
    forward.start()

    def cot_pair(x_index, index):
        blocks = pl.ds(x_index * (SEQ // 2), SEQ // 2)
        return dp_copy(cot_t.at[blocks, 1 - d], cot_p.at[blocks], index)

    cot_pairs = [cot_pair(hi_x, 0), cot_pair(1 - hi_x, 1)]
    cot_pairs[0].start()
    gg[...] += grad_part(t_x)
    turn(t_x)
    forward.wait_recv()
    turn(t_far)
    cot_pairs[1].start()

    whole(mix_recv, 0).wait_recv()
    forward_transform(mix_recv, DP, spec_m)
    inverse_transform(conv_product, DP, conv_send, sent=scatter_part(conv_send, conv_recv, 3))
    conv_recv[me] = conv_send[me]
    load_q.wait()
    total = gg[...] + grad_part(t_far)
    gg[...] = total
    gc_send[...] = to_chunks((total * q_ref[...].astype(F32)).T)
    gc_recv[me] = gc_send[me]
    scatter(gc_send, gc_recv, 2)

    cut = gated.shape[0]
    lanes = gated.shape[2]
    sources = GROUP // cut
    gated_pairs = [dp_copy(gated.at[c], gated_p.at[c], 2 + c) for c in range(cut)]
    whole(conv_recv, 3).wait_recv()
    for c in range(cut):
        cols = slice(c * lanes, (c + 1) * lanes)
        conv = from_chunks(conv_recv.at[pl.ds(c * sources, sources)]).T
        gated[c] = (q_ref[:, cols].astype(F32) * conv).astype(BF16)
        gated_pairs[c].start()
        gq_ref[:, cols] = (gg[:, cols] * conv).astype(BF16)
    stores = [store(gq_ref, gq_hbm, 1)]

    def partial(o):
        rows = jnp.concatenate([gated[c] for c in range(cut)], axis=1)
        return dot(rows, w_ref[:, pl.ds(pl.multiple_of(o * width, width), width)])

    core_send[0] = partial(t_far)
    core_send[1] = partial(t_core)
    core_copy = tp_copy(core_send, core_recv, 3, t_core)
    core_copy.start()
    across[...] = partial(t_x)
    own[...] = partial(t)

    for copy in cot_pairs:
        copy.wait_recv()
    planes = ZN // 2
    y_copies = [[] for _ in range(cut)]
    z_copies = [[] for _ in range(cut)]

    def along_y(c, src, dst):
        for step in (2, 1, 3):
            to = lax.rem(y + step, YN)
            copy = remote(
                src(to), dst(step), y_ssem.at[c, step - 1], y_rsem.at[c, step - 1], {"ctx": z * YN + to}
            )
            copy.start()
            y_copies[c].append(copy)

    def along_z(c, src, dst):
        for step in (4, 3, 5, 2, 6, 1, 7):
            to = lax.rem(z + step, ZN)
            copy = remote(
                src(to), dst(step), z_ssem.at[c, step - 1], z_rsem.at[c, step - 1], {"ctx": to * YN + y}
            )
            copy.start()
            z_copies[c].append(copy)

    def sum_of(parts):
        value = parts[0].astype(F32)
        for part in parts[1:]:
            value += part.astype(F32)
        return value

    def weights(c):
        gated_pairs[c].wait_recv()

        def weight(i, carry):
            blocks = pl.ds(i * planes * YN, planes * YN)
            mine = cot_t[blocks, d].reshape(planes * YN * half_rows, positions)
            other = cot_p[blocks].reshape(planes * YN * half_rows, positions)
            term = dot(mine, gated[c]) + dot(other, gated_p[c])
            term = term.astype(BF16).reshape(planes, YN, half_rows, lanes)
            for to in range(YN):
                w_send[c, to, pl.ds(i * planes, planes)] = term[:, to]
            return carry

        lax.fori_loop(0, 2, weight, 0)
        if c == 0:
            first_recv[z] = w_send[c, :, z]
            along_z(c, lambda to: w_send.at[c, :, to], lambda step: first_recv.at[z])
        else:
            along_y(c, lambda to: w_send.at[c, to], lambda step: w_recv.at[c - 1, step - 1])

    for c in range(cut - 1):
        weights(c)
    core_copy.wait_recv()
    x_send[...] = (across[...] + core_recv[0]).astype(BF16)
    x_copy = tp_copy(x_send, x_recv, 4, t_x)
    x_copy.start()
    whole(gc_recv, 2).wait_recv()
    forward_transform(gc_recv, DP, spec_g, False)
    inverse_transform(grad_product, DP, gm_send, False, scatter_part(gm_send, gm_recv, 4))
    gm_recv[me] = gm_send[me]
    weights(cut - 1)
    inverse_transform(taps_product, 1, fg_send, False)
    fg_recv[j] = fg_send[j]
    scatter_same(fg_send, fg_recv, 5)


    def reduce_z(c):
        for copy in z_copies[c]:
            copy.wait_recv()
        last_send[...] = sum_of([first_recv[slot] for slot in range(ZN)]).astype(BF16)
        last_recv[y] = last_send[y]
        along_y(c, lambda to: last_send.at[to], lambda step: last_recv.at[y])

    def reduce_y(c):
        for copy in y_copies[c]:
            copy.wait_recv()
        value = sum_of([w_send[c, y]] + [w_recv[c - 1, slot] for slot in range(YN - 1)])
        z_send[c - 1] = value.astype(BF16)
        z_recv[c - 1, z] = z_send[c - 1, z]
        along_z(c, lambda to: z_send.at[c - 1, to], lambda step: z_recv.at[c - 1, z])

    reduce_z(0)
    for c in range(1, cut):
        reduce_y(c)
    whole(gm_recv, 4).wait_recv()
    grad_mixed = from_chunks(gm_recv).T
    gk_ref[...] = (grad_mixed * v_ref[...].astype(F32)).astype(BF16)
    gv_ref[...] = (grad_mixed * k_ref[...].astype(F32)).astype(BF16)
    stores += [store(gk_ref, gk_hbm, 2), store(gv_ref, gv_hbm, 3)]
    whole(fg_recv, 5).wait_recv()
    fg_pair = dp_copy(fg_recv, fg_part, 2 + cut)
    fg_pair.start()
    x_copy.wait_recv()
    out_ref[...] = (own[...] + core_recv[1] + x_recv[...].astype(F32)).astype(BF16)
    stores.append(store(out_ref, out_hbm, 0))
    gf_ref[pl.ds(pl.multiple_of(d * half, half), half), :] = from_chunks(fg_recv) * factor

    d_copies = []
    for c in range(cut):
        for copy in y_copies[c] if c == 0 else z_copies[c]:
            copy.wait_recv()
        slots = [last_recv[i] for i in range(YN)] if c == 0 else [z_recv[c - 1, i] for i in range(ZN)]
        value = sum_of(slots)
        d_send[c] = value * factor
        d_copy = dp_copy(d_send.at[c], d_recv.at[c], 3 + cut + c)
        d_copy.start()
        d_copies.append(d_copy)
    fg_pair.wait_recv()
    gf_ref[pl.ds(pl.multiple_of((1 - d) * half, half), half), :] = from_chunks(fg_part) * factor
    stores.append(store(gf_ref, gf_hbm, 4))
    for c in range(cut):
        cols = slice(c * lanes, (c + 1) * lanes)
        gw_ref[pl.ds(pl.multiple_of(d * half_rows, half_rows), half_rows), cols] = d_send[c]
        d_copies[c].wait_recv()
        gw_ref[pl.ds(pl.multiple_of((1 - d) * half_rows, half_rows), half_rows), cols] = d_recv[c]
    stores.append(store(gw_ref, gw_hbm, 5))

    for copy in (cot_core, cot_x, forward, core_copy, x_copy, fg_pair):
        copy.wait_send()
    for copy in cot_pairs + gated_pairs + sum(y_copies + z_copies, []) + d_copies:
        copy.wait_send()
    for index, ref in enumerate((mix_send, fil_send, gc_send, conv_send, gm_send, fg_send)):
        whole(ref, index).wait_send()
    for copy in stores:
        copy.wait()


def hand_over(*refs):
    count = (len(refs) - 2) // 3
    sources, targets, buffers = refs[:count], refs[count : 2 * count], refs[2 * count : 3 * count]
    in_sem, out_sem = refs[3 * count :]
    loads = [pltpu.make_async_copy(sources[i], buffers[i], in_sem.at[i]) for i in range(count)]
    stores = [pltpu.make_async_copy(buffers[i], targets[i], out_sem.at[i]) for i in range(count)]
    for copy in loads:
        copy.start()
    for load, store in zip(loads, stores):
        load.wait()
        store.start()
    for copy in stores:
        copy.wait()


def local(query_proj, key_proj, value_proj, filters, w_out, cotangent):
    positions, channels = query_proj.shape[1:]
    features = w_out.shape[1] // SEQ
    half_rows = features // DP
    factor = 1.0 / math.sqrt(DP * LENGTH)
    one, back, two, twiddle = (jnp.asarray(table) for table in tables())
    stream = jax.ShapeDtypeStruct((positions, channels), BF16)
    anywhere = pl.BlockSpec(memory_space=pl.ANY)
    chunks = pltpu.VMEM((GROUP, 2 * CH, LANES), BF16)
    half_chunks = pltpu.VMEM((SEQ, 2 * CH, LANES), BF16)
    stream_buffer = pltpu.VMEM((positions, channels), BF16)
    wide_buffer = pltpu.VMEM((positions, channels), F32)
    cut = channels // LANES
    lanes = LANES
    dma = pltpu.SemaphoreType.DMA
    out_shape = (
        stream,
        stream,
        stream,
        stream,
        jax.ShapeDtypeStruct((channels, positions), F32),
        jax.ShapeDtypeStruct((features, channels), F32),
    )
    outs = pl.pallas_call(
        functools.partial(kernel, factor),
        out_shape=out_shape,
        in_specs=[anywhere] * 10,
        out_specs=[anywhere] * 6,
        scratch_shapes=[
            stream_buffer, stream_buffer, stream_buffer,
            pltpu.VMEM(filters.shape, F32),
            pltpu.VMEM(w_out.shape, BF16),
            *[pltpu.VMEM(out.shape, out.dtype) for out in out_shape],
            pltpu.VMEM(one.shape, BF16),
            pltpu.VMEM(back.shape, BF16),
            pltpu.VMEM(two.shape, BF16),
            pltpu.VMEM(twiddle.shape, F32),
            chunks, chunks, half_chunks, half_chunks, chunks, chunks,
            chunks, chunks, chunks, chunks, half_chunks, half_chunks, half_chunks,
            pltpu.VMEM((4, positions, channels), BF16),
            pltpu.VMEM((SEQ, DP, half_rows, positions), BF16),
            pltpu.VMEM((SEQ, half_rows, positions), BF16),
            wide_buffer,
            pltpu.VMEM((ROWS, DP * LANES), BF16),
            pltpu.VMEM((DP, ROWS, 2 * LANES), F32),
            pltpu.VMEM((1, ROWS, 2 * LANES), F32),
            pltpu.VMEM((DP, ROWS, 2 * LANES), F32),
            pltpu.VMEM((2 * ROWS, DP * LANES), BF16),
            pltpu.VMEM((2 * ROWS, DP * LANES), BF16),
            pltpu.VMEM((cut, positions, lanes), BF16),
            pltpu.VMEM((cut, positions, lanes), BF16),
            pltpu.VMEM((cut, YN, ZN, half_rows, lanes), BF16),
            pltpu.VMEM((cut - 1, YN - 1, ZN, half_rows, lanes), BF16),
            pltpu.VMEM((cut - 1, ZN, half_rows, lanes), BF16),
            pltpu.VMEM((cut - 1, ZN, half_rows, lanes), BF16),
            pltpu.VMEM((ZN, YN, half_rows, lanes), BF16),
            pltpu.VMEM((YN, half_rows, lanes), BF16),
            pltpu.VMEM((YN, half_rows, lanes), BF16),
            pltpu.VMEM((cut, half_rows, lanes), F32),
            pltpu.VMEM((cut, half_rows, lanes), F32),
            pltpu.VMEM((2, positions, channels), F32),
            pltpu.VMEM((2, positions, channels), F32),
            stream_buffer, stream_buffer,
            wide_buffer, wide_buffer,
            dma((10,)), dma((6,)), dma((6,)), dma((6,)), dma((5,)), dma((5,)), dma((3 + 2 * cut,)), dma((3 + 2 * cut,)),
            dma((cut, 3)), dma((cut, 3)), dma((cut, 7)), dma((cut, 7)),
        ],
        compiler_params=pltpu.CompilerParams(
            collective_id=0, has_side_effects=True, vmem_limit_bytes=56 * 1024 * 1024
        ),
        cost_estimate=pl.CostEstimate(flops=8_000_000_000, bytes_accessed=12_000_000, transcendentals=0),
    )(query_proj[0], key_proj[0], value_proj[0], filters, w_out, cotangent[0], one, back, two, twiddle)
    outs = pl.pallas_call(
        hand_over,
        out_shape=out_shape,
        in_specs=[anywhere] * 6,
        out_specs=[anywhere] * 6,
        scratch_shapes=[*[pltpu.VMEM(out.shape, out.dtype) for out in out_shape], dma((6,)), dma((6,))],
    )(*outs)
    output, grad_query, grad_key, grad_value, grad_filter, grad_wout = outs
    return (
        output[None],
        grad_query[None],
        grad_key[None],
        grad_value[None],
        grad_filter,
        grad_wout.T,
    )


def solution(mesh):
    stream = P("dp", "ctx", "tp")
    taps = P("tp", "ctx")
    return jax.shard_map(
        local,
        mesh=mesh,
        in_specs=(stream, stream, stream, taps, P("tp", None), stream),
        out_specs=(stream, stream, stream, stream, taps, taps),
        check_vma=False,
    )
```

```python
import functools
import math

import jax
import jax.numpy as jnp
import ml_dtypes
import numpy as np
from jax import lax
from jax.experimental import pallas as pl
from jax.experimental.pallas import tpu as pltpu
from jax.sharding import PartitionSpec as P

MESH = pl.DeviceIdType.MESH
F32 = jnp.float32
BF16 = jnp.bfloat16

DP = 2
SEQ = 32
ZN = 8
YN = 4
GROUP = DP * SEQ
CH = 8
BLOCKS = 64
LANES = 128
LENGTH = BLOCKS * LANES
ROWS = BLOCKS * CH
STEP = 256


def halves(table):
    high = table.astype(ml_dtypes.bfloat16)
    low = (table - high.astype(np.float64)).astype(ml_dtypes.bfloat16)
    return np.stack([high, low])


@functools.lru_cache(maxsize=None)
def tables():
    k1 = np.arange(BLOCKS)[:, None].astype(np.float64)
    turn = 2 * math.pi * k1 + math.pi / 2
    outer = turn * np.arange(BLOCKS)[None, :] / BLOCKS
    eye = np.eye(CH)
    stage_one = np.concatenate([np.kron(np.cos(outer), eye), np.kron(-np.sin(outer), eye)], axis=0)
    angle = np.repeat(turn * np.arange(LANES)[None, :] / LENGTH, CH, axis=0)
    twiddle = np.stack([np.cos(angle), -np.sin(angle)]).astype(np.float32)
    lane = np.arange(LANES)
    inner = 2 * math.pi * ((lane[:, None] * lane[None, :]) % LANES) / LANES
    c, s = np.cos(inner), np.sin(inner)
    stage_two = np.block([[c, -s], [s, c]])
    stage_two_back = np.block([[c, s], [-s, c]])
    return (
        halves(stage_one),
        halves(stage_one.T),
        np.concatenate([halves(stage_two), halves(stage_two_back)]),
        twiddle,
    )


def dot(a, b):
    return jnp.dot(a, b, preferred_element_type=F32)


def split(x):
    high = x.astype(BF16)
    return high, (x - high.astype(F32)).astype(BF16)


def kernel(
    factor,
    q_hbm, k_hbm, v_hbm, f_hbm, w_hbm, cot_hbm, one_hbm, back_hbm, two_hbm, tw_hbm,
    out_hbm, gq_hbm, gk_hbm, gv_hbm, gf_hbm, gw_hbm,
    q_ref, k_ref, v_ref, f_ref, w_ref,
    out_ref, gq_ref, gk_ref, gv_ref, gf_ref, gw_ref,
    one, back, two, tw,
    mix_send, mix_recv, fil_send, fil_recv, gc_send, gc_recv,
    conv_send, conv_recv, gm_send, gm_recv, fg_send, fg_recv, fg_part,
    cot_all, cot_t, cot_p, gg, xcat, spec_m, spec_f, spec_g, v_hi, v_lo,
    gated, gated_p, w_send, w_recv, z_send, z_recv, d_send, d_recv,
    core_send, core_recv, x_send, x_recv, own, across,
    load_sem, store_sem, send_sem, recv_sem, tp_send, tp_recv, dp_send, dp_recv,
    y_ssem, y_rsem, z_ssem, z_rsem,
):
    d = lax.axis_index("dp")
    j = lax.axis_index("ctx")
    t = lax.axis_index("tp")
    z = j // YN
    y = lax.rem(j, YN)
    core = lax.rem(t, 2)
    hi_x = t // 2
    me = d * SEQ + j
    t_core = hi_x * 2 + (1 - core)
    t_x = (1 - hi_x) * 2 + core
    t_far = (1 - hi_x) * 2 + (1 - core)

    def peer(offset):
        p = lax.rem(me + offset, GROUP)
        return p, {"dp": p // SEQ, "ctx": lax.rem(p, SEQ)}

    barrier = pltpu.get_barrier_semaphore()

    def greet(i, carry):
        pl.semaphore_signal(barrier, inc=1, device_id=peer(i)[1], device_id_type=MESH)
        return carry

    def load(src, dst, index):
        copy = pltpu.make_async_copy(src, dst, load_sem.at[index])
        copy.start()
        return copy

    def store(src, dst, index):
        copy = pltpu.make_async_copy(src, dst, store_sem.at[index])
        copy.start()
        return copy

    lax.fori_loop(1, GROUP, greet, 0, unroll=9)
    for other in (t_core, t_x):
        pl.semaphore_signal(barrier, inc=1, device_id={"tp": other}, device_id_type=MESH)
    load_f = load(f_hbm, f_ref, 0)
    load_cot = load(cot_hbm, cot_all.at[t], 3)
    load_k = load(k_hbm, k_ref, 1)
    load_v = load(v_hbm, v_ref, 2)
    load_w = load(w_hbm, w_ref, 4)
    load_q = load(q_hbm, q_ref, 5)
    load_tables = [
        load(src, dst, 6 + i)
        for i, (src, dst) in enumerate(((one_hbm, one), (two_hbm, two), (tw_hbm, tw), (back_hbm, back)))
    ]

    def to_chunks(rows):
        count = rows.shape[0] // CH
        parts = [rows[:, h * LANES : (h + 1) * LANES].reshape(count, CH, LANES) for h in range(2)]
        return jnp.concatenate(parts, axis=1).astype(BF16)

    def from_chunks(ref):
        chunks = ref[...].astype(F32)
        count = chunks.shape[0]
        parts = [chunks[:, h * CH : (h + 1) * CH, :].reshape(count * CH, LANES) for h in range(2)]
        return jnp.concatenate(parts, axis=1)

    half = SEQ * CH
    load_f.wait()
    fil_send[...] = to_chunks(f_ref[pl.ds(pl.multiple_of(d * half, half), half), :])
    fil_recv[j] = fil_send[j]
    load_cot.wait()

    pl.semaphore_wait(barrier, GROUP + 1)

    def remote(src, dst, ssem, rsem, device):
        return pltpu.make_async_remote_copy(
            src_ref=src, dst_ref=dst, send_sem=ssem, recv_sem=rsem, device_id=device, device_id_type=MESH
        )

    def tp_copy(src, dst, index, to):
        return remote(src, dst, tp_send.at[index], tp_recv.at[index], {"tp": to})

    def dp_copy(src, dst, index):
        return remote(src, dst, dp_send.at[index], dp_recv.at[index], {"dp": 1 - d})

    cot_core = tp_copy(cot_all.at[t], cot_all.at[t], 0, t_core)
    cot_x = tp_copy(cot_all.at[t], cot_all.at[t], 1, t_x)
    cot_x.start()
    cot_core.start()

    def scatter(src, dst, index, first=1, last=GROUP):
        def start(i, carry):
            p, device = peer(i)
            remote(src.at[p], dst.at[me], send_sem.at[index], recv_sem.at[index], device).start()
            return carry

        lax.fori_loop(first, last, start, 0)

    def scatter_same(src, dst, index):
        def start(i, carry):
            p = lax.rem(j + i, SEQ)
            remote(src.at[p], dst.at[j], send_sem.at[index], recv_sem.at[index], {"ctx": p}).start()
            return carry

        lax.fori_loop(1, SEQ, start, 0)

    def whole(ref, index):
        part = ref.at[pl.ds(0, ref.shape[0] - 1)]
        return remote(part, part, send_sem.at[index], recv_sem.at[index], {"tp": t_core})

    scatter_same(fil_send, fil_recv, 1)
    load_k.wait()
    load_v.wait()
    mix_send[...] = to_chunks((k_ref[...].astype(F32) * v_ref[...].astype(F32)).T)
    mix_recv[me] = mix_send[me]
    scatter(mix_send, mix_recv, 0)

    width = q_ref.shape[1]
    positions = q_ref.shape[0]
    half_rows = cot_t.shape[2]

    def grad_part(o):
        weights = w_ref[:, pl.ds(pl.multiple_of(o * width, width), width)]
        return lax.dot_general(
            cot_all[o], weights, (((1,), (1,)), ((), ())), preferred_element_type=F32
        )

    per = width // (DP * half_rows)

    def turn(o):
        turned = cot_all[o].astype(F32).T.astype(BF16)
        cot_t[pl.ds(o * per, per)] = turned.reshape(per, DP, half_rows, positions)

    def rows_of(i, base=0):
        return pl.ds(pl.multiple_of(base + i * STEP, STEP), STEP)

    def forward_transform(recv, count, spec):
        for b in range(count):
            xcat[:, b * LANES : (b + 1) * LANES] = recv[b * SEQ : (b + 1) * SEQ].reshape(ROWS, LANES)

        def body(i, carry):
            x = xcat[:, : count * LANES]
            real = dot(one[0, rows_of(i), :], x) + dot(one[1, rows_of(i), :], x)
            imag = dot(one[0, rows_of(i, ROWS), :], x) + dot(one[1, rows_of(i, ROWS), :], x)
            c, s = tw[0, rows_of(i), :], tw[1, rows_of(i), :]
            for b in range(count):
                re = real[:, b * LANES : (b + 1) * LANES]
                im = imag[:, b * LANES : (b + 1) * LANES]
                high, low = split(jnp.concatenate([re * c - im * s, re * s + im * c], axis=1))
                spec[b, rows_of(i), :] = dot(high, two[0]) + dot(low, two[0]) + dot(high, two[1])
            return carry

        lax.fori_loop(0, ROWS // STEP, body, 0, unroll=True)

    def inverse_transform(product, count, send):
        def first(i, carry):
            c, s = tw[0, rows_of(i), :], tw[1, rows_of(i), :]
            for b in range(count):
                high, low = split(jnp.concatenate(product(b, rows_of(i)), axis=1))
                u = dot(high, two[2]) + dot(low, two[2]) + dot(high, two[3])
                re, im = u[:, :LANES], u[:, LANES:]
                lanes = slice(b * LANES, (b + 1) * LANES)
                high, low = split(re * c + im * s)
                v_hi[rows_of(i), lanes] = high
                v_lo[rows_of(i), lanes] = low
                high, low = split(im * c - re * s)
                v_hi[rows_of(i, ROWS), lanes] = high
                v_lo[rows_of(i, ROWS), lanes] = low
            return carry

        lax.fori_loop(0, ROWS // STEP, first, 0, unroll=True)

        def second(i, carry):
            high, low = v_hi[:, : count * LANES], v_lo[:, : count * LANES]
            table = back[0, rows_of(i), :]
            result = dot(table, high) + dot(table, low) + dot(back[1, rows_of(i), :], high)
            result = (result * (1.0 / LENGTH)).astype(BF16)
            chunks = STEP // (2 * CH)
            for b in range(count):
                part = result[:, b * LANES : (b + 1) * LANES].reshape(chunks, 2 * CH, LANES)
                send[pl.ds(b * SEQ + i * chunks, chunks)] = part
            return carry

        lax.fori_loop(0, ROWS // STEP, second, 0, unroll=True)

    def pair(ref, b, rows):
        return ref[b, rows, :LANES], ref[b, rows, LANES:]

    def conv_product(b, rows):
        fr, fi = pair(spec_f, 0, rows)
        mr, mi = pair(spec_m, b, rows)
        return fr * mr - fi * mi, fr * mi + fi * mr

    def grad_product(b, rows):
        fr, fi = pair(spec_f, 0, rows)
        gr, gi = pair(spec_g, b, rows)
        return fr * gr + fi * gi, fr * gi - fi * gr

    def taps_product(_, rows):
        real, imag = 0.0, 0.0
        for b in range(DP):
            mr, mi = pair(spec_m, b, rows)
            gr, gi = pair(spec_g, b, rows)
            real += gr * mr + gi * mi
            imag += gi * mr - gr * mi
        return real, imag

    load_w.wait()
    gg[...] = grad_part(t)
    turn(t)
    cot_core.wait_recv()
    gg[...] += grad_part(t_core)
    turn(t_core)
    for copy in load_tables:
        copy.wait()
    whole(fil_recv, 1).wait_recv()
    forward_transform(fil_recv, 1, spec_f)
    cot_x.wait_recv()
    forward = tp_copy(cot_all.at[t_x], cot_all.at[t_x], 2, t_core)
    forward.start()

    def cot_pair(x_index, index):
        blocks = pl.ds(x_index * (SEQ // 2), SEQ // 2)
        return dp_copy(cot_t.at[blocks, 1 - d], cot_p.at[blocks], index)

    cot_pairs = [cot_pair(hi_x, 0), cot_pair(1 - hi_x, 1)]
    cot_pairs[0].start()
    gg[...] += grad_part(t_x)
    turn(t_x)
    forward.wait_recv()
    turn(t_far)
    cot_pairs[1].start()

    whole(mix_recv, 0).wait_recv()
    forward_transform(mix_recv, DP, spec_m)
    inverse_transform(conv_product, DP, conv_send)
    conv_recv[me] = conv_send[me]
    scatter(conv_send, conv_recv, 3)
    load_q.wait()
    total = gg[...] + grad_part(t_far)
    gg[...] = total
    gc_send[...] = to_chunks((total * q_ref[...].astype(F32)).T)
    gc_recv[me] = gc_send[me]
    scatter(gc_send, gc_recv, 2)

    cut = gated.shape[0]
    lanes = gated.shape[2]
    sources = GROUP // cut
    gated_pairs = [dp_copy(gated.at[c], gated_p.at[c], 2 + c) for c in range(cut)]
    whole(conv_recv, 3).wait_recv()
    for c in range(cut):
        cols = slice(c * lanes, (c + 1) * lanes)
        conv = from_chunks(conv_recv.at[pl.ds(c * sources, sources)]).T
        gated[c] = (q_ref[:, cols].astype(F32) * conv).astype(BF16)
        gated_pairs[c].start()
        gq_ref[:, cols] = (gg[:, cols] * conv).astype(BF16)
    stores = [store(gq_ref, gq_hbm, 1)]

    def partial(o):
        rows = jnp.concatenate([gated[c] for c in range(cut)], axis=1)
        return dot(rows, w_ref[:, pl.ds(pl.multiple_of(o * width, width), width)])

    core_send[0] = partial(t_far)
    core_send[1] = partial(t_core)
    core_copy = tp_copy(core_send, core_recv, 3, t_core)
    core_copy.start()
    across[...] = partial(t_x)
    own[...] = partial(t)

    for copy in cot_pairs:
        copy.wait_recv()
    planes = ZN // 2
    y_copies = []

    def weights(c):
        gated_pairs[c].wait_recv()

        def weight(i, carry):
            blocks = pl.ds(i * planes * YN, planes * YN)
            mine = cot_t[blocks, d].reshape(planes * YN * half_rows, positions)
            other = cot_p[blocks].reshape(planes * YN * half_rows, positions)
            term = dot(mine, gated[c]) + dot(other, gated_p[c])
            term = term.astype(BF16).reshape(planes, YN, half_rows, lanes)
            for to in range(YN):
                w_send[c, to, pl.ds(i * planes, planes)] = term[:, to]
            return carry

        lax.fori_loop(0, 2, weight, 0)
        for step in (2, 1, 3):
            to = lax.rem(y + step, YN)
            copy = remote(
                w_send.at[c, to], w_recv.at[c, step - 1], y_ssem.at[c, step - 1], y_rsem.at[c, step - 1],
                {"ctx": z * YN + to},
            )
            copy.start()
            y_copies.append(copy)

    for c in range(cut - 1):
        weights(c)
    core_copy.wait_recv()
    x_send[...] = (across[...] + core_recv[0]).astype(BF16)
    x_copy = tp_copy(x_send, x_recv, 4, t_x)
    x_copy.start()
    whole(gc_recv, 2).wait_recv()
    forward_transform(gc_recv, DP, spec_g)
    inverse_transform(grad_product, DP, gm_send)
    gm_recv[me] = gm_send[me]
    scatter(gm_send, gm_recv, 4)
    weights(cut - 1)
    inverse_transform(taps_product, 1, fg_send)
    fg_recv[j] = fg_send[j]
    scatter_same(fg_send, fg_recv, 5)


    z_copies = []

    def reduce_y(c):
        for copy in y_copies[c * 3 : c * 3 + 3]:
            copy.wait_recv()
        value = w_send[c, y].astype(F32)
        for slot in range(YN - 1):
            value += w_recv[c, slot].astype(F32)
        z_send[c] = value.astype(BF16)
        z_recv[c, z] = z_send[c, z]
        for step in (4, 3, 5, 2, 6, 1, 7):
            to = lax.rem(z + step, ZN)
            copy = remote(
                z_send.at[c, to], z_recv.at[c, z], z_ssem.at[c, step - 1], z_rsem.at[c, step - 1],
                {"ctx": to * YN + y},
            )
            copy.start()
            z_copies.append(copy)

    for c in range(cut):
        reduce_y(c)
    whole(gm_recv, 4).wait_recv()
    grad_mixed = from_chunks(gm_recv).T
    gk_ref[...] = (grad_mixed * v_ref[...].astype(F32)).astype(BF16)
    gv_ref[...] = (grad_mixed * k_ref[...].astype(F32)).astype(BF16)
    stores += [store(gk_ref, gk_hbm, 2), store(gv_ref, gv_hbm, 3)]
    whole(fg_recv, 5).wait_recv()
    fg_pair = dp_copy(fg_recv, fg_part, 2 + cut)
    fg_pair.start()
    x_copy.wait_recv()
    out_ref[...] = (own[...] + core_recv[1] + x_recv[...].astype(F32)).astype(BF16)
    stores.append(store(out_ref, out_hbm, 0))
    gf_ref[pl.ds(pl.multiple_of(d * half, half), half), :] = from_chunks(fg_recv) * factor

    d_copies = []
    for c in range(cut):
        for copy in z_copies[c * (ZN - 1) : (c + 1) * (ZN - 1)]:
            copy.wait_recv()
        value = z_recv[c, 0].astype(F32)
        for slot in range(1, ZN):
            value += z_recv[c, slot].astype(F32)
        d_send[c] = value * factor
        d_copy = dp_copy(d_send.at[c], d_recv.at[c], 3 + cut + c)
        d_copy.start()
        d_copies.append(d_copy)
    fg_pair.wait_recv()
    gf_ref[pl.ds(pl.multiple_of((1 - d) * half, half), half), :] = from_chunks(fg_part) * factor
    stores.append(store(gf_ref, gf_hbm, 4))
    for c in range(cut):
        cols = slice(c * lanes, (c + 1) * lanes)
        gw_ref[pl.ds(pl.multiple_of(d * half_rows, half_rows), half_rows), cols] = d_send[c]
        d_copies[c].wait_recv()
        gw_ref[pl.ds(pl.multiple_of((1 - d) * half_rows, half_rows), half_rows), cols] = d_recv[c]
    stores.append(store(gw_ref, gw_hbm, 5))

    for copy in (cot_core, cot_x, forward, core_copy, x_copy, fg_pair):
        copy.wait_send()
    for copy in cot_pairs + gated_pairs + y_copies + z_copies + d_copies:
        copy.wait_send()
    for index, ref in enumerate((mix_send, fil_send, gc_send, conv_send, gm_send, fg_send)):
        whole(ref, index).wait_send()
    for copy in stores:
        copy.wait()


def hand_over(*refs):
    count = (len(refs) - 2) // 3
    sources, targets, buffers = refs[:count], refs[count : 2 * count], refs[2 * count : 3 * count]
    in_sem, out_sem = refs[3 * count :]
    loads = [pltpu.make_async_copy(sources[i], buffers[i], in_sem.at[i]) for i in range(count)]
    stores = [pltpu.make_async_copy(buffers[i], targets[i], out_sem.at[i]) for i in range(count)]
    for copy in loads:
        copy.start()
    for load, store in zip(loads, stores):
        load.wait()
        store.start()
    for copy in stores:
        copy.wait()


def local(query_proj, key_proj, value_proj, filters, w_out, cotangent):
    positions, channels = query_proj.shape[1:]
    features = w_out.shape[1] // SEQ
    half_rows = features // DP
    factor = 1.0 / math.sqrt(DP * LENGTH)
    one, back, two, twiddle = (jnp.asarray(table) for table in tables())
    stream = jax.ShapeDtypeStruct((positions, channels), BF16)
    anywhere = pl.BlockSpec(memory_space=pl.ANY)
    chunks = pltpu.VMEM((GROUP, 2 * CH, LANES), BF16)
    half_chunks = pltpu.VMEM((SEQ, 2 * CH, LANES), BF16)
    stream_buffer = pltpu.VMEM((positions, channels), BF16)
    wide_buffer = pltpu.VMEM((positions, channels), F32)
    cut = channels // LANES
    lanes = LANES
    dma = pltpu.SemaphoreType.DMA
    out_shape = (
        stream,
        stream,
        stream,
        stream,
        jax.ShapeDtypeStruct((channels, positions), F32),
        jax.ShapeDtypeStruct((features, channels), F32),
    )
    outs = pl.pallas_call(
        functools.partial(kernel, factor),
        out_shape=out_shape,
        in_specs=[anywhere] * 10,
        out_specs=[anywhere] * 6,
        scratch_shapes=[
            stream_buffer, stream_buffer, stream_buffer,
            pltpu.VMEM(filters.shape, F32),
            pltpu.VMEM(w_out.shape, BF16),
            *[pltpu.VMEM(out.shape, out.dtype) for out in out_shape],
            pltpu.VMEM(one.shape, BF16),
            pltpu.VMEM(back.shape, BF16),
            pltpu.VMEM(two.shape, BF16),
            pltpu.VMEM(twiddle.shape, F32),
            chunks, chunks, half_chunks, half_chunks, chunks, chunks,
            chunks, chunks, chunks, chunks, half_chunks, half_chunks, half_chunks,
            pltpu.VMEM((4, positions, channels), BF16),
            pltpu.VMEM((SEQ, DP, half_rows, positions), BF16),
            pltpu.VMEM((SEQ, half_rows, positions), BF16),
            wide_buffer,
            pltpu.VMEM((ROWS, DP * LANES), BF16),
            pltpu.VMEM((DP, ROWS, 2 * LANES), F32),
            pltpu.VMEM((1, ROWS, 2 * LANES), F32),
            pltpu.VMEM((DP, ROWS, 2 * LANES), F32),
            pltpu.VMEM((2 * ROWS, DP * LANES), BF16),
            pltpu.VMEM((2 * ROWS, DP * LANES), BF16),
            pltpu.VMEM((cut, positions, lanes), BF16),
            pltpu.VMEM((cut, positions, lanes), BF16),
            pltpu.VMEM((cut, YN, ZN, half_rows, lanes), BF16),
            pltpu.VMEM((cut, YN - 1, ZN, half_rows, lanes), BF16),
            pltpu.VMEM((cut, ZN, half_rows, lanes), BF16),
            pltpu.VMEM((cut, ZN, half_rows, lanes), BF16),
            pltpu.VMEM((cut, half_rows, lanes), F32),
            pltpu.VMEM((cut, half_rows, lanes), F32),
            pltpu.VMEM((2, positions, channels), F32),
            pltpu.VMEM((2, positions, channels), F32),
            stream_buffer, stream_buffer,
            wide_buffer, wide_buffer,
            dma((10,)), dma((6,)), dma((6,)), dma((6,)), dma((5,)), dma((5,)), dma((3 + 2 * cut,)), dma((3 + 2 * cut,)),
            dma((cut, 3)), dma((cut, 3)), dma((cut, 7)), dma((cut, 7)),
        ],
        compiler_params=pltpu.CompilerParams(
            collective_id=0, has_side_effects=True, vmem_limit_bytes=56 * 1024 * 1024
        ),
        cost_estimate=pl.CostEstimate(flops=8_000_000_000, bytes_accessed=12_000_000, transcendentals=0),
    )(query_proj[0], key_proj[0], value_proj[0], filters, w_out, cotangent[0], one, back, two, twiddle)
    outs = pl.pallas_call(
        hand_over,
        out_shape=out_shape,
        in_specs=[anywhere] * 6,
        out_specs=[anywhere] * 6,
        scratch_shapes=[*[pltpu.VMEM(out.shape, out.dtype) for out in out_shape], dma((6,)), dma((6,))],
    )(*outs)
    output, grad_query, grad_key, grad_value, grad_filter, grad_wout = outs
    return (
        output[None],
        grad_query[None],
        grad_key[None],
        grad_value[None],
        grad_filter,
        grad_wout.T,
    )


def solution(mesh):
    stream = P("dp", "ctx", "tp")
    taps = P("tp", "ctx")
    return jax.shard_map(
        local,
        mesh=mesh,
        in_specs=(stream, stream, stream, taps, P("tp", None), stream),
        out_specs=(stream, stream, stream, stream, taps, taps),
        check_vma=False,
    )
```

```python
import functools
import math

import jax
import jax.numpy as jnp
import ml_dtypes
import numpy as np
from jax import lax
from jax.experimental import pallas as pl
from jax.experimental.pallas import tpu as pltpu
from jax.sharding import PartitionSpec as P

MESH = pl.DeviceIdType.MESH
F32 = jnp.float32
BF16 = jnp.bfloat16

DP = 2
SEQ = 32
ZN = 8
YN = 4
GROUP = DP * SEQ
CH = 8
BLOCKS = 64
LANES = 128
LENGTH = BLOCKS * LANES
ROWS = BLOCKS * CH
STEP = 256


def halves(table):
    high = table.astype(ml_dtypes.bfloat16)
    low = (table - high.astype(np.float64)).astype(ml_dtypes.bfloat16)
    return np.stack([high, low])


@functools.lru_cache(maxsize=None)
def tables():
    k1 = np.arange(BLOCKS)[:, None].astype(np.float64)
    turn = 2 * math.pi * k1 + math.pi / 2
    outer = turn * np.arange(BLOCKS)[None, :] / BLOCKS
    eye = np.eye(CH)
    stage_one = np.concatenate([np.kron(np.cos(outer), eye), np.kron(-np.sin(outer), eye)], axis=0)
    angle = np.repeat(turn * np.arange(LANES)[None, :] / LENGTH, CH, axis=0)
    twiddle = np.stack([np.cos(angle), -np.sin(angle)]).astype(np.float32)
    lane = np.arange(LANES)
    inner = 2 * math.pi * ((lane[:, None] * lane[None, :]) % LANES) / LANES
    c, s = np.cos(inner), np.sin(inner)
    stage_two = np.block([[c, -s], [s, c]])
    stage_two_back = np.block([[c, s], [-s, c]])
    return (
        halves(stage_one),
        halves(stage_one.T),
        np.concatenate([halves(stage_two), halves(stage_two_back)]),
        twiddle,
    )


def dot(a, b):
    return jnp.dot(a, b, preferred_element_type=F32)


def split(x):
    high = x.astype(BF16)
    return high, (x - high.astype(F32)).astype(BF16)


def kernel(
    factor,
    q_hbm, k_hbm, v_hbm, f_hbm, w_hbm, cot_hbm, one_hbm, back_hbm, two_hbm, tw_hbm,
    out_hbm, gq_hbm, gk_hbm, gv_hbm, gf_hbm, gw_hbm,
    q_ref, k_ref, v_ref, f_ref, w_ref,
    out_ref, gq_ref, gk_ref, gv_ref, gf_ref, gw_ref,
    one, back, two, tw,
    mix_send, mix_recv, fil_send, fil_recv, gc_send, gc_recv,
    conv_send, conv_recv, gm_send, gm_recv, fg_send, fg_recv, fg_part,
    cot_all, cot_t, cot_p, gg, xcat, spec_m, spec_f, spec_g, v_hi, v_lo,
    gated, gated_p, w_send, w_recv, z_send, z_recv, d_send, d_recv,
    core_send, core_recv, x_send, x_recv, own, across,
    load_sem, store_sem, send_sem, recv_sem, tp_send, tp_recv, dp_send, dp_recv,
    y_ssem, y_rsem, z_ssem, z_rsem,
):
    d = lax.axis_index("dp")
    j = lax.axis_index("ctx")
    t = lax.axis_index("tp")
    z = j // YN
    y = lax.rem(j, YN)
    core = lax.rem(t, 2)
    hi_x = t // 2
    me = d * SEQ + j
    t_core = hi_x * 2 + (1 - core)
    t_x = (1 - hi_x) * 2 + core
    t_far = (1 - hi_x) * 2 + (1 - core)

    def peer(offset):
        p = lax.rem(me + offset, GROUP)
        return p, {"dp": p // SEQ, "ctx": lax.rem(p, SEQ)}

    barrier = pltpu.get_barrier_semaphore()

    def greet(i, carry):
        far_first = lax.rem(i + GROUP // 4 - 2, GROUP - 1) + 1
        pl.semaphore_signal(barrier, inc=1, device_id=peer(far_first)[1], device_id_type=MESH)
        return carry

    def load(src, dst, index):
        copy = pltpu.make_async_copy(src, dst, load_sem.at[index])
        copy.start()
        return copy

    def store(src, dst, index):
        copy = pltpu.make_async_copy(src, dst, store_sem.at[index])
        copy.start()
        return copy

    lax.fori_loop(1, GROUP, greet, 0, unroll=9)
    for other in (t_core, t_x):
        pl.semaphore_signal(barrier, inc=1, device_id={"tp": other}, device_id_type=MESH)
    load_f = load(f_hbm, f_ref, 0)
    load_cot = load(cot_hbm, cot_all.at[t], 3)
    load_k = load(k_hbm, k_ref, 1)
    load_v = load(v_hbm, v_ref, 2)
    load_w = load(w_hbm, w_ref, 4)
    load_q = load(q_hbm, q_ref, 5)
    load_tables = [
        load(src, dst, 6 + i)
        for i, (src, dst) in enumerate(((one_hbm, one), (two_hbm, two), (tw_hbm, tw), (back_hbm, back)))
    ]

    def to_chunks(rows):
        count = rows.shape[0] // CH
        parts = [rows[:, h * LANES : (h + 1) * LANES].reshape(count, CH, LANES) for h in range(2)]
        return jnp.concatenate(parts, axis=1).astype(BF16)

    def from_chunks(ref):
        chunks = ref[...].astype(F32)
        count = chunks.shape[0]
        parts = [chunks[:, h * CH : (h + 1) * CH, :].reshape(count * CH, LANES) for h in range(2)]
        return jnp.concatenate(parts, axis=1)

    half = SEQ * CH
    load_f.wait()
    fil_send[...] = to_chunks(f_ref[pl.ds(pl.multiple_of(d * half, half), half), :])
    fil_recv[j] = fil_send[j]
    load_cot.wait()

    pl.semaphore_wait(barrier, GROUP + 1)

    def remote(src, dst, ssem, rsem, device):
        return pltpu.make_async_remote_copy(
            src_ref=src, dst_ref=dst, send_sem=ssem, recv_sem=rsem, device_id=device, device_id_type=MESH
        )

    def tp_copy(src, dst, index, to):
        return remote(src, dst, tp_send.at[index], tp_recv.at[index], {"tp": to})

    def dp_copy(src, dst, index):
        return remote(src, dst, dp_send.at[index], dp_recv.at[index], {"dp": 1 - d})

    cot_core = tp_copy(cot_all.at[t], cot_all.at[t], 0, t_core)
    cot_x = tp_copy(cot_all.at[t], cot_all.at[t], 1, t_x)
    cot_x.start()
    cot_core.start()

    def scatter(src, dst, index, first=1, last=GROUP):
        def start(i, carry):
            p, device = peer(i)
            remote(src.at[p], dst.at[me], send_sem.at[index], recv_sem.at[index], device).start()
            return carry

        lax.fori_loop(first, last, start, 0)

    def scatter_same(src, dst, index):
        def start(i, carry):
            p = lax.rem(j + i, SEQ)
            remote(src.at[p], dst.at[j], send_sem.at[index], recv_sem.at[index], {"ctx": p}).start()
            return carry

        lax.fori_loop(1, SEQ, start, 0)

    def whole(ref, index):
        part = ref.at[pl.ds(0, ref.shape[0] - 1)]
        return remote(part, part, send_sem.at[index], recv_sem.at[index], {"tp": t_core})

    scatter_same(fil_send, fil_recv, 1)
    load_k.wait()
    load_v.wait()
    mix_send[...] = to_chunks((k_ref[...].astype(F32) * v_ref[...].astype(F32)).T)
    mix_recv[me] = mix_send[me]
    scatter(mix_send, mix_recv, 0)

    width = q_ref.shape[1]
    positions = q_ref.shape[0]
    half_rows = cot_t.shape[2]

    def grad_part(o):
        weights = w_ref[:, pl.ds(pl.multiple_of(o * width, width), width)]
        return lax.dot_general(
            cot_all[o], weights, (((1,), (1,)), ((), ())), preferred_element_type=F32
        )

    per = width // (DP * half_rows)

    def turn(o):
        turned = cot_all[o].astype(F32).T.astype(BF16)
        cot_t[pl.ds(o * per, per)] = turned.reshape(per, DP, half_rows, positions)

    def rows_of(i, base=0):
        return pl.ds(pl.multiple_of(base + i * STEP, STEP), STEP)

    def forward_transform(recv, count, spec):
        for b in range(count):
            xcat[:, b * LANES : (b + 1) * LANES] = recv[b * SEQ : (b + 1) * SEQ].reshape(ROWS, LANES)

        def body(i, carry):
            x = xcat[:, : count * LANES]
            real = dot(one[0, rows_of(i), :], x) + dot(one[1, rows_of(i), :], x)
            imag = dot(one[0, rows_of(i, ROWS), :], x) + dot(one[1, rows_of(i, ROWS), :], x)
            c, s = tw[0, rows_of(i), :], tw[1, rows_of(i), :]
            for b in range(count):
                re = real[:, b * LANES : (b + 1) * LANES]
                im = imag[:, b * LANES : (b + 1) * LANES]
                high, low = split(jnp.concatenate([re * c - im * s, re * s + im * c], axis=1))
                spec[b, rows_of(i), :] = dot(high, two[0]) + dot(low, two[0]) + dot(high, two[1])
            return carry

        lax.fori_loop(0, ROWS // STEP, body, 0, unroll=True)

    def inverse_transform(product, count, send):
        def first(i, carry):
            c, s = tw[0, rows_of(i), :], tw[1, rows_of(i), :]
            for b in range(count):
                high, low = split(jnp.concatenate(product(b, rows_of(i)), axis=1))
                u = dot(high, two[2]) + dot(low, two[2]) + dot(high, two[3])
                re, im = u[:, :LANES], u[:, LANES:]
                lanes = slice(b * LANES, (b + 1) * LANES)
                high, low = split(re * c + im * s)
                v_hi[rows_of(i), lanes] = high
                v_lo[rows_of(i), lanes] = low
                high, low = split(im * c - re * s)
                v_hi[rows_of(i, ROWS), lanes] = high
                v_lo[rows_of(i, ROWS), lanes] = low
            return carry

        lax.fori_loop(0, ROWS // STEP, first, 0, unroll=True)

        def second(i, carry):
            high, low = v_hi[:, : count * LANES], v_lo[:, : count * LANES]
            table = back[0, rows_of(i), :]
            result = dot(table, high) + dot(table, low) + dot(back[1, rows_of(i), :], high)
            result = (result * (1.0 / LENGTH)).astype(BF16)
            chunks = STEP // (2 * CH)
            for b in range(count):
                part = result[:, b * LANES : (b + 1) * LANES].reshape(chunks, 2 * CH, LANES)
                send[pl.ds(b * SEQ + i * chunks, chunks)] = part
            return carry

        lax.fori_loop(0, ROWS // STEP, second, 0, unroll=True)

    def pair(ref, b, rows):
        return ref[b, rows, :LANES], ref[b, rows, LANES:]

    def conv_product(b, rows):
        fr, fi = pair(spec_f, 0, rows)
        mr, mi = pair(spec_m, b, rows)
        return fr * mr - fi * mi, fr * mi + fi * mr

    def grad_product(b, rows):
        fr, fi = pair(spec_f, 0, rows)
        gr, gi = pair(spec_g, b, rows)
        return fr * gr + fi * gi, fr * gi - fi * gr

    def taps_product(_, rows):
        real, imag = 0.0, 0.0
        for b in range(DP):
            mr, mi = pair(spec_m, b, rows)
            gr, gi = pair(spec_g, b, rows)
            real += gr * mr + gi * mi
            imag += gi * mr - gr * mi
        return real, imag

    load_w.wait()
    gg[...] = grad_part(t)
    turn(t)
    cot_core.wait_recv()
    gg[...] += grad_part(t_core)
    turn(t_core)
    for copy in load_tables:
        copy.wait()
    whole(fil_recv, 1).wait_recv()
    forward_transform(fil_recv, 1, spec_f)
    cot_x.wait_recv()
    forward = tp_copy(cot_all.at[t_x], cot_all.at[t_x], 2, t_core)
    forward.start()

    def cot_pair(x_index, index):
        blocks = pl.ds(x_index * (SEQ // 2), SEQ // 2)
        return dp_copy(cot_t.at[blocks, 1 - d], cot_p.at[blocks], index)

    cot_pairs = [cot_pair(hi_x, 0), cot_pair(1 - hi_x, 1)]
    cot_pairs[0].start()
    gg[...] += grad_part(t_x)
    turn(t_x)
    forward.wait_recv()
    turn(t_far)
    cot_pairs[1].start()

    whole(mix_recv, 0).wait_recv()
    forward_transform(mix_recv, DP, spec_m)
    inverse_transform(conv_product, DP, conv_send)
    conv_recv[me] = conv_send[me]
    scatter(conv_send, conv_recv, 3)
    load_q.wait()
    total = gg[...] + grad_part(t_far)
    gg[...] = total
    gc_send[...] = to_chunks((total * q_ref[...].astype(F32)).T)
    gc_recv[me] = gc_send[me]
    scatter(gc_send, gc_recv, 2)

    cut = gated.shape[0]
    lanes = gated.shape[2]
    sources = GROUP // cut
    gated_pairs = [dp_copy(gated.at[c], gated_p.at[c], 2 + c) for c in range(cut)]
    whole(conv_recv, 3).wait_recv()
    for c in range(cut):
        cols = slice(c * lanes, (c + 1) * lanes)
        conv = from_chunks(conv_recv.at[pl.ds(c * sources, sources)]).T
        gated[c] = (q_ref[:, cols].astype(F32) * conv).astype(BF16)
        gated_pairs[c].start()
        gq_ref[:, cols] = (gg[:, cols] * conv).astype(BF16)
    stores = [store(gq_ref, gq_hbm, 1)]

    def partial(o):
        rows = jnp.concatenate([gated[c] for c in range(cut)], axis=1)
        return dot(rows, w_ref[:, pl.ds(pl.multiple_of(o * width, width), width)])

    core_send[0] = partial(t_far)
    core_send[1] = partial(t_core)
    core_copy = tp_copy(core_send, core_recv, 3, t_core)
    core_copy.start()
    across[...] = partial(t_x)
    own[...] = partial(t)

    for copy in cot_pairs:
        copy.wait_recv()
    planes = ZN // 2
    y_copies = []

    def weights(c):
        gated_pairs[c].wait_recv()

        def weight(i, carry):
            blocks = pl.ds(i * planes * YN, planes * YN)
            mine = cot_t[blocks, d].reshape(planes * YN * half_rows, positions)
            other = cot_p[blocks].reshape(planes * YN * half_rows, positions)
            term = dot(mine, gated[c]) + dot(other, gated_p[c])
            term = term.astype(BF16).reshape(planes, YN, half_rows, lanes)
            for to in range(YN):
                w_send[c, to, pl.ds(i * planes, planes)] = term[:, to]
            return carry

        lax.fori_loop(0, 2, weight, 0, unroll=True)
        for step in (2, 1, 3):
            to = lax.rem(y + step, YN)
            copy = remote(
                w_send.at[c, to], w_recv.at[c, step - 1], y_ssem.at[c, step - 1], y_rsem.at[c, step - 1],
                {"ctx": z * YN + to},
            )
            copy.start()
            y_copies.append(copy)

    for c in range(cut - 1):
        weights(c)
    core_copy.wait_recv()
    x_send[...] = (across[...] + core_recv[0]).astype(BF16)
    x_copy = tp_copy(x_send, x_recv, 4, t_x)
    x_copy.start()
    whole(gc_recv, 2).wait_recv()
    forward_transform(gc_recv, DP, spec_g)
    inverse_transform(grad_product, DP, gm_send)
    gm_recv[me] = gm_send[me]
    scatter(gm_send, gm_recv, 4)
    weights(cut - 1)
    inverse_transform(taps_product, 1, fg_send)
    fg_recv[j] = fg_send[j]
    scatter_same(fg_send, fg_recv, 5)


    z_copies = []

    def reduce_y(c):
        for copy in y_copies[c * 3 : c * 3 + 3]:
            copy.wait_recv()
        value = w_send[c, y].astype(F32)
        for slot in range(YN - 1):
            value += w_recv[c, slot].astype(F32)
        z_send[c] = value.astype(BF16)
        z_recv[c, z] = z_send[c, z]
        for step in (4, 3, 5, 2, 6, 1, 7):
            to = lax.rem(z + step, ZN)
            copy = remote(
                z_send.at[c, to], z_recv.at[c, z], z_ssem.at[c, step - 1], z_rsem.at[c, step - 1],
                {"ctx": to * YN + y},
            )
            copy.start()
            z_copies.append(copy)

    for c in range(cut):
        reduce_y(c)
    whole(gm_recv, 4).wait_recv()
    grad_mixed = from_chunks(gm_recv).T
    gk_ref[...] = (grad_mixed * v_ref[...].astype(F32)).astype(BF16)
    gv_ref[...] = (grad_mixed * k_ref[...].astype(F32)).astype(BF16)
    stores += [store(gk_ref, gk_hbm, 2), store(gv_ref, gv_hbm, 3)]
    whole(fg_recv, 5).wait_recv()
    fg_pair = dp_copy(fg_recv, fg_part, 2 + cut)
    fg_pair.start()
    x_copy.wait_recv()
    out_ref[...] = (own[...] + core_recv[1] + x_recv[...].astype(F32)).astype(BF16)
    stores.append(store(out_ref, out_hbm, 0))
    gf_ref[pl.ds(pl.multiple_of(d * half, half), half), :] = from_chunks(fg_recv) * factor

    d_copies = []
    for c in range(cut):
        for copy in z_copies[c * (ZN - 1) : (c + 1) * (ZN - 1)]:
            copy.wait_recv()
        value = z_recv[c, 0].astype(F32)
        for slot in range(1, ZN):
            value += z_recv[c, slot].astype(F32)
        d_send[c] = value * factor
        d_copy = dp_copy(d_send.at[c], d_recv.at[c], 3 + cut + c)
        d_copy.start()
        d_copies.append(d_copy)
    fg_pair.wait_recv()
    gf_ref[pl.ds(pl.multiple_of((1 - d) * half, half), half), :] = from_chunks(fg_part) * factor
    stores.append(store(gf_ref, gf_hbm, 4))
    for c in range(cut):
        cols = slice(c * lanes, (c + 1) * lanes)
        gw_ref[pl.ds(pl.multiple_of(d * half_rows, half_rows), half_rows), cols] = d_send[c]
        d_copies[c].wait_recv()
        gw_ref[pl.ds(pl.multiple_of((1 - d) * half_rows, half_rows), half_rows), cols] = d_recv[c]
    stores.append(store(gw_ref, gw_hbm, 5))

    for copy in (cot_core, cot_x, forward, core_copy, x_copy, fg_pair):
        copy.wait_send()
    for copy in cot_pairs + gated_pairs + y_copies + z_copies + d_copies:
        copy.wait_send()
    for index, ref in enumerate((mix_send, fil_send, gc_send, conv_send, gm_send, fg_send)):
        whole(ref, index).wait_send()
    for copy in stores:
        copy.wait()


def hand_over(*refs):
    count = (len(refs) - 2) // 3
    sources, targets, buffers = refs[:count], refs[count : 2 * count], refs[2 * count : 3 * count]
    in_sem, out_sem = refs[3 * count :]
    loads = [pltpu.make_async_copy(sources[i], buffers[i], in_sem.at[i]) for i in range(count)]
    stores = [pltpu.make_async_copy(buffers[i], targets[i], out_sem.at[i]) for i in range(count)]
    for copy in loads:
        copy.start()
    for load, store in zip(loads, stores):
        load.wait()
        store.start()
    for copy in stores:
        copy.wait()


def local(query_proj, key_proj, value_proj, filters, w_out, cotangent):
    positions, channels = query_proj.shape[1:]
    features = w_out.shape[1] // SEQ
    half_rows = features // DP
    factor = 1.0 / math.sqrt(DP * LENGTH)
    one, back, two, twiddle = (jnp.asarray(table) for table in tables())
    stream = jax.ShapeDtypeStruct((positions, channels), BF16)
    anywhere = pl.BlockSpec(memory_space=pl.ANY)
    chunks = pltpu.VMEM((GROUP, 2 * CH, LANES), BF16)
    half_chunks = pltpu.VMEM((SEQ, 2 * CH, LANES), BF16)
    stream_buffer = pltpu.VMEM((positions, channels), BF16)
    wide_buffer = pltpu.VMEM((positions, channels), F32)
    cut = channels // LANES
    lanes = LANES
    dma = pltpu.SemaphoreType.DMA
    out_shape = (
        stream,
        stream,
        stream,
        stream,
        jax.ShapeDtypeStruct((channels, positions), F32),
        jax.ShapeDtypeStruct((features, channels), F32),
    )
    outs = pl.pallas_call(
        functools.partial(kernel, factor),
        out_shape=out_shape,
        in_specs=[anywhere] * 10,
        out_specs=[anywhere] * 6,
        scratch_shapes=[
            stream_buffer, stream_buffer, stream_buffer,
            pltpu.VMEM(filters.shape, F32),
            pltpu.VMEM(w_out.shape, BF16),
            *[pltpu.VMEM(out.shape, out.dtype) for out in out_shape],
            pltpu.VMEM(one.shape, BF16),
            pltpu.VMEM(back.shape, BF16),
            pltpu.VMEM(two.shape, BF16),
            pltpu.VMEM(twiddle.shape, F32),
            chunks, chunks, half_chunks, half_chunks, chunks, chunks,
            chunks, chunks, chunks, chunks, half_chunks, half_chunks, half_chunks,
            pltpu.VMEM((4, positions, channels), BF16),
            pltpu.VMEM((SEQ, DP, half_rows, positions), BF16),
            pltpu.VMEM((SEQ, half_rows, positions), BF16),
            wide_buffer,
            pltpu.VMEM((ROWS, DP * LANES), BF16),
            pltpu.VMEM((DP, ROWS, 2 * LANES), F32),
            pltpu.VMEM((1, ROWS, 2 * LANES), F32),
            pltpu.VMEM((DP, ROWS, 2 * LANES), F32),
            pltpu.VMEM((2 * ROWS, DP * LANES), BF16),
            pltpu.VMEM((2 * ROWS, DP * LANES), BF16),
            pltpu.VMEM((cut, positions, lanes), BF16),
            pltpu.VMEM((cut, positions, lanes), BF16),
            pltpu.VMEM((cut, YN, ZN, half_rows, lanes), BF16),
            pltpu.VMEM((cut, YN - 1, ZN, half_rows, lanes), BF16),
            pltpu.VMEM((cut, ZN, half_rows, lanes), BF16),
            pltpu.VMEM((cut, ZN, half_rows, lanes), BF16),
            pltpu.VMEM((cut, half_rows, lanes), F32),
            pltpu.VMEM((cut, half_rows, lanes), F32),
            pltpu.VMEM((2, positions, channels), F32),
            pltpu.VMEM((2, positions, channels), F32),
            stream_buffer, stream_buffer,
            wide_buffer, wide_buffer,
            dma((10,)), dma((6,)), dma((6,)), dma((6,)), dma((5,)), dma((5,)), dma((3 + 2 * cut,)), dma((3 + 2 * cut,)),
            dma((cut, 3)), dma((cut, 3)), dma((cut, 7)), dma((cut, 7)),
        ],
        compiler_params=pltpu.CompilerParams(
            collective_id=0, has_side_effects=True, vmem_limit_bytes=56 * 1024 * 1024
        ),
        cost_estimate=pl.CostEstimate(flops=8_000_000_000, bytes_accessed=12_000_000, transcendentals=0),
    )(query_proj[0], key_proj[0], value_proj[0], filters, w_out, cotangent[0], one, back, two, twiddle)
    outs = pl.pallas_call(
        hand_over,
        out_shape=out_shape,
        in_specs=[anywhere] * 6,
        out_specs=[anywhere] * 6,
        scratch_shapes=[*[pltpu.VMEM(out.shape, out.dtype) for out in out_shape], dma((6,)), dma((6,))],
    )(*outs)
    output, grad_query, grad_key, grad_value, grad_filter, grad_wout = outs
    return (
        output[None],
        grad_query[None],
        grad_key[None],
        grad_value[None],
        grad_filter,
        grad_wout.T,
    )


def solution(mesh):
    stream = P("dp", "ctx", "tp")
    taps = P("tp", "ctx")
    return jax.shard_map(
        local,
        mesh=mesh,
        in_specs=(stream, stream, stream, taps, P("tp", None), stream),
        out_specs=(stream, stream, stream, stream, taps, taps),
        check_vma=False,
    )
```
